32 devices in a mesh: patch: 2 (over y), tile: 8 (over z, core), row: 2 (over x), band: 1.
Axes of the slice: x: 2, y: 2, z: 4, core: 2. Of those that a mesh axis runs over, the one named last changes fastest.
Arguments:
- stamps: bfloat16 [768, 64, 128], P(('patch', 'tile', 'row', 'band')), parts along dimension 0, may hold values from -6 to 6
- variance: bfloat16 [768, 64, 128], P(('patch', 'tile', 'row', 'band')), parts along dimension 0, may hold values from 0.25 to 4
- basis_v: bfloat16 [21, 41], replicated, may hold values from -1 to 1
- basis_u: bfloat16 [21, 41], replicated, may hold values from -1 to 1
- coefficients: float32 [800, 21], P('patch'), parts along dimension 0, may hold values from 0.03 to 0.3
- coef_index: int32 [768], P(('patch', 'tile', 'row', 'band')), parts along dimension 0, may hold values from 0 to 399
- tile_dest: int32 [768], P(('patch', 'tile', 'row', 'band')), parts along dimension 0, may hold values from 0 to 7, as said below
- row_offset: int32 [768], P(('patch', 'tile', 'row', 'band')), parts along dimension 0, may hold values from 0 to 448
- sub_pixel: int32 [768, 2], P(('patch', 'tile', 'row', 'band')), parts along dimension 0, may hold values from 0 to 63
Outputs:
- coadd: float32 [8192, 128], P(('patch', 'tile', 'row', 'band')), parts along dimension 0
The draws below stay inside these ranges and needn't reach their ends.
There are 2 independent parts, one for each index of `patch`. The reference program is written for one: setup_inputs(seed, part) draws one part's arguments, and reference() takes and returns one part's arrays. A program takes and returns all parts, laid end to end along the dimension named above; an argument that names none is the same for every part. Nothing has to cross between parts.
Inputs may be any that keep to these rules, and one draw needn't show every extreme that they name: `tile_dest`: among the 24 stamps of one device at most 3 name the same tile, and one tile is named by exactly 3 stamps of every device.
All inputs are finite; a program needn't handle non-finite values.
Results may differ from the reference program's by a relative error of at most 0.0055.
Values may be sent and summed in bfloat16 or wider, within the bound.
A program may use at most 64 MiB of HBM per device.

```python
import math
import jax
import jax.numpy as jnp
from jax import lax

SH = 64
SW = 128
TAPS = 41
NB = 21
SUBSTEPS = 64
EXPOSURES = 400
STAMP_DEV = 24
TILE_ROWS = 512
CAP = 3
N_STAMP = 384
COADD_ROWS = 4096
N_TILE = 8


def draw_tile_dest(key, part):
    key_hot, key_rest = jax.random.split(key)
    hot_tile = jax.random.randint(key_hot, (), 0, N_TILE)
    others = (hot_tile + 1 + jnp.arange(N_TILE - 1)) % N_TILE
    others_pool = jnp.repeat(others, CAP)
    block_count = N_STAMP // STAMP_DEV

    def one_block(block_key):
        key_pick, key_order = jax.random.split(block_key)
        picks = jax.random.permutation(key_pick, others_pool)[:STAMP_DEV - CAP]
        listed = jnp.concatenate([jnp.zeros((CAP,), jnp.int32) + hot_tile, picks.astype(jnp.int32)])
        return jax.random.permutation(key_order, listed)
    blocks = jax.vmap(one_block)(jax.random.split(key_rest, block_count))
    return blocks.reshape(-1).astype(jnp.int32)


def set_ends(drawn, own_key, smallest, top_value):
    extent = drawn.shape
    place = [jax.random.randint(jax.random.fold_in(own_key, axis), (), 0, extent[axis]) for axis in range(len(extent))]
    drawn = drawn.at[tuple(place)].set(smallest)
    longest = extent.index(max(extent))
    place[longest] = (place[longest] + 1) % extent[longest]
    return drawn.at[tuple(place)].set(top_value)


def block_scale(own_key, shape, shards, smallest, high):
    def one(position, shards_of):
        steps = jax.random.uniform(jax.random.fold_in(jax.random.fold_in(own_key, 6), position), (shards_of,), jnp.float32, smallest / len(shards), high / len(shards))
        return jnp.repeat(jnp.exp(steps), shape[position] // shards_of).reshape((-1,) + (1,) * (len(shape) - position - 1))

    level = one(*shards[0])
    for cut in shards[1:]:
        level = level * one(*cut)
    return level


def centred(rng, dims, width, reach, cuts=(), kind=jnp.bfloat16):
    array = jax.random.normal(rng, dims, jnp.float32) * width
    if len(cuts) > 0:
        array = block_scale(rng, dims, cuts, -0.22, 0.18) * array
    return jnp.clip(array, min=-reach, max=reach).astype(kind)


def setup_inputs(seed: int = 0, part: int = 0) -> dict:
    arg_keys = jax.random.split(jax.random.key(seed), 10)
    own_keys = jax.random.split(jax.random.fold_in(arg_keys[9], part), 10)
    stamps = centred(own_keys[0], (N_STAMP, SH, SW), 1.0, 6.0, ((0, 16),))
    variance = jnp.clip(jnp.exp(math.log(4.0) - 2.7725887 * jax.random.uniform(own_keys[1], (N_STAMP, SH, SW), jnp.float32) ** block_scale(own_keys[1], (N_STAMP, SH, SW), ((0, 16),), -0.2, 0.2)), 0.25, 4.0).astype(jnp.bfloat16)
    basis_v = centred(arg_keys[2], (NB, TAPS), TAPS ** -0.5, 1.0)
    basis_u = centred(arg_keys[3], (NB, TAPS), TAPS ** -0.5, 1.0)
    coefficients = jnp.clip(jnp.exp(jax.random.uniform(own_keys[4], (EXPOSURES, NB), jnp.float32, math.log(0.03), math.log(0.3))), 0.03, 0.3)
    coef_index = set_ends(jax.random.randint(own_keys[5], (N_STAMP,), 0, EXPOSURES), jax.random.fold_in(own_keys[5], 1), 0, EXPOSURES - 1).astype(jnp.int32)
    tile_dest = draw_tile_dest(jax.random.fold_in(jax.random.fold_in(arg_keys[9], part), 71), part)
    row_offset = set_ends(jax.random.randint(own_keys[7], (N_STAMP,), 0, TILE_ROWS - SH + 1), jax.random.fold_in(own_keys[7], 1), 0, TILE_ROWS - SH).astype(jnp.int32)
    sub_pixel = set_ends(jax.random.randint(own_keys[8], (N_STAMP, 2), 0, SUBSTEPS), jax.random.fold_in(own_keys[8], 1), 0, SUBSTEPS - 1).astype(jnp.int32)
    return dict(stamps=stamps, variance=variance, basis_v=basis_v, basis_u=basis_u, coefficients=coefficients, coef_index=coef_index, tile_dest=tile_dest, row_offset=row_offset, sub_pixel=sub_pixel)


def band_tables(basis_v, basis_u, stamp_rows, stamp_cols):
    tap_count = basis_v.shape[1]
    half_width = (tap_count - 1) // 2
    row_ids = jnp.arange(stamp_rows).astype(jnp.int32)
    col_ids = jnp.arange(stamp_cols).astype(jnp.int32)
    tap_ids = jnp.arange(tap_count).astype(jnp.int32)
    lag_rows = row_ids[None, :] - row_ids[:, None] + half_width
    pick_rows = (lag_rows[None, :, :] == tap_ids[:, None, None]).astype(jnp.float32)
    vertical = jnp.einsum("ka,aij->kij", basis_v.astype(jnp.float32), pick_rows,
                          precision=lax.Precision.HIGHEST).astype(jnp.bfloat16)
    lag_cols = col_ids[:, None] - col_ids[None, :] + half_width
    pick_cols = (lag_cols[None, :, :] == tap_ids[:, None, None]).astype(jnp.float32)
    horizontal = jnp.einsum("ka,apq->pkq", basis_u.astype(jnp.float32), pick_cols,
                            precision=lax.Precision.HIGHEST).astype(jnp.bfloat16)
    return vertical, horizontal.reshape(stamp_cols, -1)


def bilinear(values, frac_rows, frac_cols):
    below = jnp.concatenate([values[:, 1:], values[:, -1:]], axis=1)
    mixed = (1.0 - frac_rows) * values + frac_rows * below
    beside = jnp.concatenate([mixed[:, :, 1:], mixed[:, :, -1:]], axis=2)
    return (1.0 - frac_cols) * mixed + frac_cols * beside


def reference(stamps, variance, basis_v, basis_u, coefficients, coef_index, tile_dest, row_offset, sub_pixel):
    stamp_total, stamp_rows, stamp_cols = stamps.shape
    nbasis = basis_v.shape[0]
    vertical, horiz_table = band_tables(basis_v, basis_u, stamp_rows, stamp_cols)
    group_size = math.gcd(stamp_total, 64)
    groups = stamp_total // group_size
    coef_all = coefficients[coef_index.astype(jnp.int32)]
    row_ids = jnp.arange(stamp_rows).astype(jnp.int32)

    def step(carry, operands):
        numer_all, denom_all = carry
        images, spreads, coef_part, dest, offset, shift = operands
        flattened = images.reshape(group_size * stamp_rows, stamp_cols)
        horizontal = jnp.dot(flattened, horiz_table, preferred_element_type=jnp.float32).astype(jnp.bfloat16)
        horizontal = horizontal.reshape(group_size, stamp_rows, nbasis, stamp_cols)
        vertical_out = jnp.einsum("kai,bikc->bkac", vertical.astype(jnp.float32), horizontal.astype(jnp.float32),
                                  precision=lax.Precision.HIGHEST)
        matched = jnp.sum(coef_part[:, :, None, None] * vertical_out, axis=1).astype(jnp.bfloat16)
        frac_rows = shift[:, 0].astype(jnp.float32)[:, None, None] / SUBSTEPS
        frac_cols = shift[:, 1].astype(jnp.float32)[:, None, None] / SUBSTEPS
        warped = bilinear(matched.astype(jnp.float32), frac_rows, frac_cols)
        spread = bilinear(spreads.astype(jnp.float32), frac_rows, frac_cols)
        weight = 1.0 / spread
        rows_at = (dest.astype(jnp.int32) * TILE_ROWS + offset.astype(jnp.int32))[:, None] + row_ids[None, :]
        rows_flat = rows_at.reshape(-1)
        numer_all = numer_all.at[rows_flat].add((weight * warped).reshape(-1, stamp_cols))
        denom_all = denom_all.at[rows_flat].add(weight.reshape(-1, stamp_cols))
        return (numer_all, denom_all), None

    start = (jnp.zeros((COADD_ROWS, stamp_cols), jnp.float32), jnp.zeros((COADD_ROWS, stamp_cols), jnp.float32))
    operands = (stamps.reshape(groups, group_size, stamp_rows, stamp_cols),
                variance.reshape(groups, group_size, stamp_rows, stamp_cols),
                coef_all.reshape(groups, group_size, nbasis),
                tile_dest.reshape(groups, group_size),
                row_offset.reshape(groups, group_size),
                sub_pixel.reshape(groups, group_size, 2))
    (numer_all, denom_all), _ = lax.scan(step, start, operands)
    return numer_all / (denom_all + 1.0)
```

```python
import functools

import jax
import jax.numpy as jnp
from jax import lax
from jax.experimental import pallas as pl
from jax.experimental.pallas import tpu as pltpu
from jax.sharding import PartitionSpec as P

SUBSTEPS = 64
TILE_ROWS = 512
MESH = pl.DeviceIdType.MESH


def largest_divisor(value, limit):
    return max(d for d in range(1, limit + 1) if value % d == 0)


def paired(index, step, count):
    if count & (count - 1):
        return lax.rem(index + step, count)
    total, bit = 0, 1
    while bit < count:
        digit = lax.rem(lax.div(index, bit), 2) + lax.rem(lax.div(step, bit), 2)
        total = total + lax.rem(digit, 2) * bit
        bit *= 2
    return total


def kernel(
    sizes,
    stamps, variance, basis_v, basis_u, coef, coef_index, tile_dest, row_offset, sub_pixel,
    out,
    taps_v, taps_u, vtab, utab, tmat, send_x, send_m, recv_x, recv_m, acc, part_s, part_r,
    sx_sem, rx_sem, sm_sem, rm_sem, sp_sem, rp_sem,
):
    tiles, rows_n, bands, cap = sizes
    count, sh, sw = stamps.shape
    nb, tap_count = basis_v.shape
    half = (tap_count - 1) // 2
    owners = rows_n * bands
    own_rows = TILE_ROWS // owners
    me = lax.axis_index("tile")
    mine = lax.axis_index("row") * bands + lax.axis_index("band")

    def owner_id(q):
        peer = lax.rem(mine + q, owners)
        return peer, {"row": lax.div(peer, bands), "band": lax.rem(peer, bands)}

    barrier = pltpu.get_barrier_semaphore()
    for step in range(1, tiles):
        pl.semaphore_signal(
            barrier, inc=1, device_id={"tile": lax.rem(me + step, tiles)}, device_id_type=MESH
        )
    for q in range(1, owners):
        pl.semaphore_signal(barrier, inc=1, device_id=owner_id(q)[1], device_id_type=MESH)

    taps_v[...] = jnp.zeros_like(taps_v)
    taps_u[...] = jnp.zeros_like(taps_u)
    taps_v[0:nb, 0:tap_count] = basis_v[...].astype(jnp.float32)
    taps_u[0:nb, 0:tap_count] = basis_u[...].astype(jnp.float32)
    taps_v[...] = pltpu.roll(taps_v[...], sw - half, 1)
    taps_u[...] = pltpu.roll(taps_u[...], sw - half, 1)
    lag = lax.broadcasted_iota(jnp.int32, (sw, sw), 1) - lax.broadcasted_iota(jnp.int32, (sw, sw), 0)
    near = jnp.abs(lag) <= half
    for k in range(nb):
        line = jnp.broadcast_to(taps_v[k : k + 1, :], (sh, sw))
        rolled = pltpu.roll(line, 0, 1, stride=1, stride_axis=0)
        vtab[k * sh : (k + 1) * sh, :] = rolled[:, :sh].astype(jnp.bfloat16)
        line = jnp.broadcast_to(taps_u[k : k + 1, :], (sw, sw))
        rolled = pltpu.roll(line, 0, 1, stride=1, stride_axis=0)
        utab[k * sw : (k + 1) * sw, :] = jnp.where(near, rolled, 0.0).T.astype(jnp.bfloat16)

    pl.semaphore_wait(barrier, tiles - 1 + owners - 1)

    last_row = lax.broadcasted_iota(jnp.int32, (sh, sw), 0) == sh - 1
    last_col = lax.broadcasted_iota(jnp.int32, (sh, sw), 1) == sw - 1
    width = send_m.shape[2]
    lane = lax.broadcasted_iota(jnp.int32, (1, width), 1)
    chunk = largest_divisor(nb, 7)

    def bilinear(values, frac_rows, frac_cols):
        below = jnp.where(last_row, values, pltpu.roll(values, sh - 1, 0))
        mixed = (1.0 - frac_rows) * values + frac_rows * below
        beside = jnp.where(last_col, mixed, pltpu.roll(mixed, sw - 1, 1))
        return (1.0 - frac_cols) * mixed + frac_cols * beside

    def data_copy(step):
        return pltpu.make_async_remote_copy(
            src_ref=send_x.at[step], dst_ref=recv_x.at[step],
            send_sem=sx_sem.at[step], recv_sem=rx_sem.at[step],
            device_id={"tile": paired(me, step, tiles)}, device_id_type=MESH,
        )

    def place_copy(step):
        return pltpu.make_async_remote_copy(
            src_ref=send_m.at[step], dst_ref=recv_m.at[step],
            send_sem=sm_sem.at[step], recv_sem=rm_sem.at[step],
            device_id={"tile": paired(me, step, tiles)}, device_id_type=MESH,
        )

    def produce(step):
        dst = paired(me, step, tiles)
        listed = jnp.int32(0)
        for s in range(count):
            listed = jnp.where(tile_dest[s] == dst, listed * (count + 1) + (s + 1), listed)
        picks, live = [], []
        for r in range(cap):
            digit = lax.rem(listed, count + 1)
            listed = lax.div(listed, count + 1)
            picks.append(jnp.maximum(digit - 1, 0))
            live.append(digit > 0)
        images = jnp.concatenate([stamps[p] for p in picks], axis=1)
        weights = [coef[pl.ds(coef_index[p], 1), :] for p in picks]
        for base in range(0, nb, chunk):
            part = jnp.dot(
                vtab[base * sh : (base + chunk) * sh, :], images, preferred_element_type=jnp.float32
            )
            for k in range(chunk):
                for r in range(cap):
                    block = part[k * sh : (k + 1) * sh, r * sw : (r + 1) * sw]
                    scale = weights[r][:, base + k : base + k + 1]
                    tmat[r * sh : (r + 1) * sh, (base + k) * sw : (base + k + 1) * sw] = (
                        block * scale
                    ).astype(jnp.bfloat16)
        matched = jnp.dot(tmat[...], utab[...], preferred_element_type=jnp.float32)
        matched = matched.astype(jnp.bfloat16).astype(jnp.float32)
        place = jnp.full((1, width), -1, jnp.int32)
        for r in range(cap):
            p = picks[r]
            frac_rows = sub_pixel[p, 0].astype(jnp.float32) * (1.0 / SUBSTEPS)
            frac_cols = sub_pixel[p, 1].astype(jnp.float32) * (1.0 / SUBSTEPS)
            warped = bilinear(matched[r * sh : (r + 1) * sh, :], frac_rows, frac_cols)
            spread = bilinear(variance[p].astype(jnp.float32), frac_rows, frac_cols)
            weight = 1.0 / spread
            send_x[step, r * sh : (r + 1) * sh, 0:sw] = (weight * warped).astype(jnp.bfloat16)
            send_x[step, r * sh : (r + 1) * sh, sw : 2 * sw] = weight.astype(jnp.bfloat16)
            first = jnp.where(live[r], row_offset[p], -4 * TILE_ROWS)
            inside = (lane >= r * sh) & (lane < (r + 1) * sh)
            place = jnp.where(inside, first + lane - r * sh, place)
        send_m[step] = place

    def send_one(i, carry):
        step = tiles - 1 - i
        produce(step)
        data_copy(step).start()
        place_copy(step).start()
        return carry

    lax.fori_loop(0, tiles - 1, send_one, 0)
    produce(0)

    row_ids = lax.broadcasted_iota(jnp.int32, (TILE_ROWS, cap * sh), 0)

    def landed(block, place):
        picks = jnp.where(row_ids == place[:, : cap * sh], 1.0, 0.0).astype(jnp.bfloat16)
        return jnp.dot(picks, block, preferred_element_type=jnp.float32)

    acc[...] = landed(send_x[0], send_m[0])

    def take_one(i, carry):
        step = jnp.where(i < tiles // 2, i, tiles - 1 - (i - tiles // 2))
        data_copy(step).wait_recv()
        place_copy(step).wait_recv()
        acc[...] += landed(recv_x[step], recv_m[step])
        return carry

    lax.fori_loop(1, tiles, take_one, 0)

    def part_copy(q):
        return pltpu.make_async_remote_copy(
            src_ref=part_s.at[q], dst_ref=part_r.at[q],
            send_sem=sp_sem.at[q], recv_sem=rp_sem.at[q],
            device_id=owner_id(q)[1], device_id_type=MESH,
        )

    for q in range(1, owners):
        peer = owner_id(q)[0]
        start = pl.multiple_of(peer * own_rows, own_rows)
        part_s[q] = acc[pl.ds(start, own_rows), :].astype(jnp.bfloat16)
        part_copy(q).start()
    start = pl.multiple_of(mine * own_rows, own_rows)
    total = acc[pl.ds(start, own_rows), :]
    for q in range(1, owners):
        part_copy(q).wait_recv()
        total = total + part_r[q].astype(jnp.float32)
    out[...] = total[:, :sw] / (total[:, sw:] + 1.0)

    def drain(step, carry):
        data_copy(step).wait_send()
        place_copy(step).wait_send()
        return carry

    lax.fori_loop(1, tiles, drain, 0)
    for q in range(1, owners):
        part_copy(q).wait_send()


def local(
    stamps, variance, basis_v, basis_u, coefficients, coef_index, tile_dest, row_offset, sub_pixel
):
    tiles = lax.axis_size("tile")
    rows_n = lax.axis_size("row")
    bands = lax.axis_size("band")
    count, sh, sw = stamps.shape
    nb = basis_v.shape[0]
    cap = max(2, (count + tiles - 1) // tiles)
    owners = rows_n * bands
    own_rows = TILE_ROWS // owners
    width = -(-cap * sh // 128) * 128
    vmem = pl.BlockSpec(memory_space=pltpu.VMEM)
    smem = pl.BlockSpec(memory_space=pltpu.SMEM)
    nb_pad = -(-nb // 8) * 8
    bf16, f32 = jnp.bfloat16, jnp.float32
    return pl.pallas_call(
        functools.partial(kernel, (tiles, rows_n, bands, cap)),
        out_shape=jax.ShapeDtypeStruct((own_rows, sw), f32),
        in_specs=[vmem] * 5 + [smem] * 4,
        out_specs=vmem,
        scratch_shapes=[
            pltpu.VMEM((nb_pad, sw), f32),
            pltpu.VMEM((nb_pad, sw), f32),
            pltpu.VMEM((nb * sh, sh), bf16),
            pltpu.VMEM((nb * sw, sw), bf16),
            pltpu.VMEM((cap * sh, nb * sw), bf16),
            pltpu.VMEM((tiles, cap * sh, 2 * sw), bf16),
            pltpu.VMEM((tiles, 1, width), jnp.int32),
            pltpu.VMEM((tiles, cap * sh, 2 * sw), bf16),
            pltpu.VMEM((tiles, 1, width), jnp.int32),
            pltpu.VMEM((TILE_ROWS, 2 * sw), f32),
            pltpu.VMEM((owners, own_rows, 2 * sw), bf16),
            pltpu.VMEM((owners, own_rows, 2 * sw), bf16),
            pltpu.SemaphoreType.DMA((tiles,)),
            pltpu.SemaphoreType.DMA((tiles,)),
            pltpu.SemaphoreType.DMA((tiles,)),
            pltpu.SemaphoreType.DMA((tiles,)),
            pltpu.SemaphoreType.DMA((owners,)),
            pltpu.SemaphoreType.DMA((owners,)),
        ],
        compiler_params=pltpu.CompilerParams(
            collective_id=0, has_side_effects=True, vmem_limit_bytes=48 * 1024 * 1024
        ),
    )(stamps, variance, basis_v, basis_u, coefficients, coef_index, tile_dest, row_offset, sub_pixel)


def solution(mesh):
    in_specs = (
        P(("patch", "tile", "row", "band"), None, None),
        P(("patch", "tile", "row", "band"), None, None),
        P(),
        P(),
        P("patch", None),
        P(("patch", "tile", "row", "band")),
        P(("patch", "tile", "row", "band")),
        P(("patch", "tile", "row", "band")),
        P(("patch", "tile", "row", "band"), None),
    )
    out_specs = P(("patch", "tile", "row", "band"), None)
    return jax.shard_map(local, mesh=mesh, in_specs=in_specs, out_specs=out_specs, check_vma=False)
```

```python
import functools

import jax
import jax.numpy as jnp
from jax import lax
from jax.experimental import pallas as pl
from jax.experimental.pallas import tpu as pltpu
from jax.sharding import PartitionSpec as P

SUBSTEPS = 64
TILE_ROWS = 512
MESH = pl.DeviceIdType.MESH


def largest_divisor(value, limit):
    return max(d for d in range(1, limit + 1) if value % d == 0)


def paired(index, step, count):
    if count & (count - 1):
        return lax.rem(index + step, count)
    total, bit = 0, 1
    while bit < count:
        digit = lax.rem(lax.div(index, bit), 2) + lax.rem(lax.div(step, bit), 2)
        total = total + lax.rem(digit, 2) * bit
        bit *= 2
    return total


def kernel(
    sizes,
    stamps_h, variance_h, basis_v_h, basis_u_h, coef_h, index_h, dest_h, offset_h, pixel_h,
    out,
    stamps, variance, basis_v, basis_u, coef, coef_index, tile_dest, row_offset, sub_pixel,
    taps_v, taps_u, vtab, utab, tmat, send_x, send_m, recv_x, recv_m, acc, part_s, part_r,
    in_sem, sx_sem, rx_sem, sm_sem, rm_sem, sp_sem, rp_sem,
):
    loads = [
        pltpu.make_async_copy(src, dst, in_sem.at[i])
        for i, (src, dst) in enumerate(
            [
                (basis_v_h, basis_v), (basis_u_h, basis_u), (stamps_h, stamps), (coef_h, coef),
                (dest_h, tile_dest), (index_h, coef_index), (offset_h, row_offset),
                (pixel_h, sub_pixel), (variance_h, variance),
            ]
        )
    ]
    for load in loads:
        load.start()
    tiles, rows_n, bands, cap = sizes
    count, sh, sw = stamps.shape
    nb, tap_count = basis_v.shape
    half = (tap_count - 1) // 2
    owners = rows_n * bands
    own_rows = TILE_ROWS // owners
    me = lax.axis_index("tile")
    mine = lax.axis_index("row") * bands + lax.axis_index("band")

    def owner_id(q):
        peer = lax.rem(mine + q, owners)
        return peer, {"row": lax.div(peer, bands), "band": lax.rem(peer, bands)}

    barrier = pltpu.get_barrier_semaphore()
    for step in range(1, tiles):
        pl.semaphore_signal(
            barrier, inc=1, device_id={"tile": lax.rem(me + step, tiles)}, device_id_type=MESH
        )
    for q in range(1, owners):
        pl.semaphore_signal(barrier, inc=1, device_id=owner_id(q)[1], device_id_type=MESH)

    tap_ids = lax.broadcasted_iota(jnp.int32, (tap_count, sw), 0)
    lag_ids = lax.broadcasted_iota(jnp.int32, (tap_count, sw), 1)
    lag_ids = jnp.where(lag_ids > half, lag_ids - sw, lag_ids)
    forward = jnp.where(tap_ids == lag_ids + half, 1.0, 0.0).astype(jnp.bfloat16)
    mirrored = jnp.where(tap_ids == half - lag_ids, 1.0, 0.0).astype(jnp.bfloat16)
    loads[0].wait()
    taps_v[...] = jnp.dot(basis_v[...], forward, preferred_element_type=jnp.float32)
    loads[1].wait()
    taps_u[...] = jnp.dot(basis_u[...], mirrored, preferred_element_type=jnp.float32)
    lag = lax.broadcasted_iota(jnp.int32, (sw, sw), 1) - lax.broadcasted_iota(jnp.int32, (sw, sw), 0)
    near = jnp.abs(lag) <= half
    for k in range(nb):
        line = jnp.broadcast_to(taps_v[k : k + 1, :], (sh, sw))
        rolled = pltpu.roll(line, 0, 1, stride=1, stride_axis=0)
        vtab[k * sh : (k + 1) * sh, :] = rolled[:, :sh].astype(jnp.bfloat16)
        line = jnp.broadcast_to(taps_u[k : k + 1, :], (sw, sw))
        rolled = pltpu.roll(line, 0, 1, stride=1, stride_axis=0)
        utab[k * sw : (k + 1) * sw, :] = jnp.where(near, rolled, 0.0).astype(jnp.bfloat16)

    for load in loads[2:]:
        load.wait()
    pl.semaphore_wait(barrier, tiles - 1 + owners - 1)

    last_row = lax.broadcasted_iota(jnp.int32, (sh, sw), 0) == sh - 1
    last_col = lax.broadcasted_iota(jnp.int32, (sh, sw), 1) == sw - 1
    width = send_m.shape[2]
    lane = lax.broadcasted_iota(jnp.int32, (1, width), 1)
    chunk = largest_divisor(nb, 7)
    digit_bits = count.bit_length()
    exposure_ids = lax.broadcasted_iota(jnp.int32, coef.shape, 1)

    def bilinear(values, frac_rows, frac_cols):
        below = jnp.where(last_row, values, pltpu.roll(values, sh - 1, 0))
        mixed = (1.0 - frac_rows) * values + frac_rows * below
        beside = jnp.where(last_col, mixed, pltpu.roll(mixed, sw - 1, 1))
        return (1.0 - frac_cols) * mixed + frac_cols * beside

    def data_copy(step):
        return pltpu.make_async_remote_copy(
            src_ref=send_x.at[step], dst_ref=recv_x.at[step],
            send_sem=sx_sem.at[step], recv_sem=rx_sem.at[step],
            device_id={"tile": paired(me, step, tiles)}, device_id_type=MESH,
        )

    def place_copy(step):
        return pltpu.make_async_remote_copy(
            src_ref=send_m.at[step], dst_ref=recv_m.at[step],
            send_sem=sm_sem.at[step], recv_sem=rm_sem.at[step],
            device_id={"tile": paired(me, step, tiles)}, device_id_type=MESH,
        )

    def produce(step):
        dst = paired(me, step, tiles)
        listed = jnp.int32(0)
        for s in range(count):
            listed = jnp.where(tile_dest[s] == dst, (listed << digit_bits) + (s + 1), listed)
        picks, live = [], []
        for r in range(cap):
            digit = listed & ((1 << digit_bits) - 1)
            listed = listed >> digit_bits
            picks.append(jnp.maximum(digit - 1, 0))
            live.append(digit > 0)
        images = jnp.concatenate([stamps[p] for p in picks], axis=1)
        weights = [
            jnp.sum(jnp.where(exposure_ids == coef_index[p], coef[...], 0.0), axis=1, keepdims=True)
            for p in picks
        ]
        for base in range(0, nb, chunk):
            part = jnp.dot(
                vtab[base * sh : (base + chunk) * sh, :], images, preferred_element_type=jnp.float32
            )
            for k in range(chunk):
                for r in range(cap):
                    block = part[k * sh : (k + 1) * sh, r * sw : (r + 1) * sw]
                    scale = weights[r][base + k : base + k + 1, :]
                    tmat[r * sh : (r + 1) * sh, (base + k) * sw : (base + k + 1) * sw] = (
                        block * scale
                    ).astype(jnp.bfloat16)
        matched = jnp.dot(tmat[...], utab[...], preferred_element_type=jnp.float32)
        matched = matched.astype(jnp.bfloat16).astype(jnp.float32)
        place = jnp.full((1, width), -1, jnp.int32)
        for r in range(cap):
            p = picks[r]
            frac_rows = sub_pixel[0, p].astype(jnp.float32) * (1.0 / SUBSTEPS)
            frac_cols = sub_pixel[1, p].astype(jnp.float32) * (1.0 / SUBSTEPS)
            warped = bilinear(matched[r * sh : (r + 1) * sh, :], frac_rows, frac_cols)
            spread = bilinear(variance[p].astype(jnp.float32), frac_rows, frac_cols)
            weight = 1.0 / spread
            send_x[step, r * sh : (r + 1) * sh, 0:sw] = (weight * warped).astype(jnp.bfloat16)
            send_x[step, r * sh : (r + 1) * sh, sw : 2 * sw] = weight.astype(jnp.bfloat16)
            first = jnp.where(live[r], row_offset[p], -4 * TILE_ROWS)
            inside = (lane >= r * sh) & (lane < (r + 1) * sh)
            place = jnp.where(inside, first + lane - r * sh, place)
        send_m[step] = place

    def send_one(i, carry):
        step = tiles - 1 - i
        produce(step)
        data_copy(step).start()
        place_copy(step).start()
        return carry

    lax.fori_loop(0, tiles - 1, send_one, 0)
    produce(0)

    row_ids = lax.broadcasted_iota(jnp.int32, (TILE_ROWS, cap * sh), 0)

    def landed(block, place):
        picks = jnp.where(row_ids == place[:, : cap * sh], 1.0, 0.0).astype(jnp.bfloat16)
        return jnp.dot(picks, block, preferred_element_type=jnp.float32)

    acc[...] = landed(send_x[0], send_m[0])

    def take_one(i, carry):
        step = jnp.where(i < tiles // 2, i, tiles - 1 - (i - tiles // 2))
        data_copy(step).wait_recv()
        place_copy(step).wait_recv()
        acc[...] += landed(recv_x[step], recv_m[step])
        return carry

    lax.fori_loop(1, tiles, take_one, 0)

    def part_copy(q):
        return pltpu.make_async_remote_copy(
            src_ref=part_s.at[q], dst_ref=part_r.at[q],
            send_sem=sp_sem.at[q], recv_sem=rp_sem.at[q],
            device_id=owner_id(q)[1], device_id_type=MESH,
        )

    for q in range(1, owners):
        peer = owner_id(q)[0]
        start = pl.multiple_of(peer * own_rows, own_rows)
        part_s[q] = acc[pl.ds(start, own_rows), :].astype(jnp.bfloat16)
        part_copy(q).start()
    start = pl.multiple_of(mine * own_rows, own_rows)
    total = acc[pl.ds(start, own_rows), :]
    for q in range(1, owners):
        part_copy(q).wait_recv()
        total = total + part_r[q].astype(jnp.float32)
    out[...] = total[:, :sw] / (total[:, sw:] + 1.0)

    def drain(step, carry):
        data_copy(step).wait_send()
        place_copy(step).wait_send()
        return carry

    lax.fori_loop(1, tiles, drain, 0)
    for q in range(1, owners):
        part_copy(q).wait_send()


def local(
    stamps, variance, basis_v, basis_u, coefficients, coef_index, tile_dest, row_offset, sub_pixel
):
    tiles = lax.axis_size("tile")
    rows_n = lax.axis_size("row")
    bands = lax.axis_size("band")
    count, sh, sw = stamps.shape
    nb = basis_v.shape[0]
    cap = max(2, (count + tiles - 1) // tiles)
    owners = rows_n * bands
    own_rows = TILE_ROWS // owners
    width = -(-cap * sh // 128) * 128
    vmem = pl.BlockSpec(memory_space=pltpu.VMEM)
    anywhere = pl.BlockSpec(memory_space=pl.ANY)
    coefficients, sub_pixel = coefficients.T, sub_pixel.T
    big = [stamps, variance, basis_v, basis_u, coefficients]
    small = [coef_index, tile_dest, row_offset, sub_pixel]
    bf16, f32 = jnp.bfloat16, jnp.float32
    return pl.pallas_call(
        functools.partial(kernel, (tiles, rows_n, bands, cap)),
        out_shape=jax.ShapeDtypeStruct((own_rows, sw), f32),
        in_specs=[anywhere] * 9,
        out_specs=vmem,
        scratch_shapes=[
            *(pltpu.VMEM(x.shape, x.dtype) for x in big),
            *(pltpu.SMEM(x.shape, x.dtype) for x in small),
            pltpu.VMEM((nb, sw), f32),
            pltpu.VMEM((nb, sw), f32),
            pltpu.VMEM((nb * sh, sh), bf16),
            pltpu.VMEM((nb * sw, sw), bf16),
            pltpu.VMEM((cap * sh, nb * sw), bf16),
            pltpu.VMEM((tiles, cap * sh, 2 * sw), bf16),
            pltpu.VMEM((tiles, 1, width), jnp.int32),
            pltpu.VMEM((tiles, cap * sh, 2 * sw), bf16),
            pltpu.VMEM((tiles, 1, width), jnp.int32),
            pltpu.VMEM((TILE_ROWS, 2 * sw), f32),
            pltpu.VMEM((owners, own_rows, 2 * sw), bf16),
            pltpu.VMEM((owners, own_rows, 2 * sw), bf16),
            pltpu.SemaphoreType.DMA((9,)),
            pltpu.SemaphoreType.DMA((tiles,)),
            pltpu.SemaphoreType.DMA((tiles,)),
            pltpu.SemaphoreType.DMA((tiles,)),
            pltpu.SemaphoreType.DMA((tiles,)),
            pltpu.SemaphoreType.DMA((owners,)),
            pltpu.SemaphoreType.DMA((owners,)),
        ],
        compiler_params=pltpu.CompilerParams(
            collective_id=0, has_side_effects=True, vmem_limit_bytes=56 * 1024 * 1024
        ),
    )(*big, *small)


def solution(mesh):
    in_specs = (
        P(("patch", "tile", "row", "band"), None, None),
        P(("patch", "tile", "row", "band"), None, None),
        P(),
        P(),
        P("patch", None),
        P(("patch", "tile", "row", "band")),
        P(("patch", "tile", "row", "band")),
        P(("patch", "tile", "row", "band")),
        P(("patch", "tile", "row", "band"), None),
    )
    out_specs = P(("patch", "tile", "row", "band"), None)
    return jax.shard_map(local, mesh=mesh, in_specs=in_specs, out_specs=out_specs, check_vma=False)
```

```python
import functools

import jax
import jax.numpy as jnp
from jax import lax
from jax.experimental import pallas as pl
from jax.experimental.pallas import tpu as pltpu
from jax.sharding import PartitionSpec as P

SUBSTEPS = 64
TILE_ROWS = 512
MESH = pl.DeviceIdType.MESH


def largest_divisor(value, limit):
    return max(d for d in range(1, limit + 1) if value % d == 0)


def paired(index, step, count):
    if count & (count - 1):
        return lax.rem(index + step, count)
    total, bit = 0, 1
    while bit < count:
        digit = lax.rem(lax.div(index, bit), 2) + lax.rem(lax.div(step, bit), 2)
        total = total + lax.rem(digit, 2) * bit
        bit *= 2
    return total


def start_loads(sems, *pairs):
    loads = [pltpu.make_async_copy(src, dst, sems.at[i]) for i, (src, dst) in enumerate(pairs)]
    for load in loads:
        load.start()
    return loads


def bilinear_of(sh, sw):
    last_row = lax.broadcasted_iota(jnp.int32, (sh, sw), 0) == sh - 1
    last_col = lax.broadcasted_iota(jnp.int32, (sh, sw), 1) == sw - 1

    def bilinear(values, frac_rows, frac_cols):
        below = jnp.where(last_row, values, pltpu.roll(values, sh - 1, 0))
        mixed = (1.0 - frac_rows) * values + frac_rows * below
        beside = jnp.where(last_col, mixed, pltpu.roll(mixed, sw - 1, 1))
        return (1.0 - frac_cols) * mixed + frac_cols * beside

    return bilinear


def listed_stamps(tile_dest, dst, count, cap):
    bits = count.bit_length()
    listed = jnp.int32(0)
    for s in range(count):
        listed = jnp.where(tile_dest[s] == dst, (listed << bits) + (s + 1), listed)
    picks, live = [], []
    for r in range(cap):
        digit = listed & ((1 << bits) - 1)
        listed = listed >> bits
        picks.append(jnp.maximum(digit - 1, 0))
        live.append(digit > 0)
    return picks, live


def fill_tables(loads, basis_v, basis_u, taps_v, taps_u, vtab, utab, sh, sw):
    nb, tap_count = basis_v.shape
    half = (tap_count - 1) // 2
    tap_ids = lax.broadcasted_iota(jnp.int32, (tap_count, sw), 0)
    lag_ids = lax.broadcasted_iota(jnp.int32, (tap_count, sw), 1)
    lag_ids = jnp.where(lag_ids > half, lag_ids - sw, lag_ids)
    forward = jnp.where(tap_ids == lag_ids + half, 1.0, 0.0).astype(jnp.bfloat16)
    mirrored = jnp.where(tap_ids == half - lag_ids, 1.0, 0.0).astype(jnp.bfloat16)
    loads[0].wait()
    taps_v[...] = jnp.dot(basis_v[...], forward, preferred_element_type=jnp.float32)
    loads[1].wait()
    taps_u[...] = jnp.dot(basis_u[...], mirrored, preferred_element_type=jnp.float32)
    lag = lax.broadcasted_iota(jnp.int32, (sw, sw), 1) - lax.broadcasted_iota(jnp.int32, (sw, sw), 0)
    near = jnp.abs(lag) <= half
    for k in range(nb):
        line = jnp.broadcast_to(taps_v[k : k + 1, :], (sh, sw))
        rolled = pltpu.roll(line, 0, 1, stride=1, stride_axis=0)
        vtab[k * sh : (k + 1) * sh, :] = rolled[:, :sh].astype(jnp.bfloat16)
        line = jnp.broadcast_to(taps_u[k : k + 1, :], (sw, sw))
        rolled = pltpu.roll(line, 0, 1, stride=1, stride_axis=0)
        utab[k * sw : (k + 1) * sw, :] = jnp.where(near, rolled, 0.0).astype(jnp.bfloat16)


def kernel(
    sizes,
    stamps_h, variance_h, basis_v_h, basis_u_h, coef_h, index_h, dest_h, offset_h, pixel_h,
    out,
    stamps, variance, basis_v, basis_u, coef, coef_index, tile_dest, row_offset, sub_pixel,
    taps_v, taps_u, vtab, utab, tmat, send_x, send_m, recv_x, recv_m, acc, part_s, part_r,
    in_sem, sx_sem, rx_sem, sm_sem, rm_sem, sp_sem, rp_sem,
):
    loads = start_loads(
        in_sem,
        (basis_v_h, basis_v), (basis_u_h, basis_u), (stamps_h, stamps), (coef_h, coef),
        (dest_h, tile_dest), (index_h, coef_index), (offset_h, row_offset),
        (pixel_h, sub_pixel), (variance_h, variance),
    )
    tiles, rows_n, bands, cap = sizes
    count, sh, sw = stamps.shape
    nb, tap_count = basis_v.shape
    half = (tap_count - 1) // 2
    owners = rows_n * bands
    own_rows = TILE_ROWS // owners
    me = lax.axis_index("tile")
    mine = lax.axis_index("row") * bands + lax.axis_index("band")

    def owner_id(q):
        peer = lax.rem(mine + q, owners)
        return peer, {"row": lax.div(peer, bands), "band": lax.rem(peer, bands)}

    barrier = pltpu.get_barrier_semaphore()
    for step in range(1, tiles):
        pl.semaphore_signal(
            barrier, inc=1, device_id={"tile": lax.rem(me + step, tiles)}, device_id_type=MESH
        )
    for q in range(1, owners):
        pl.semaphore_signal(barrier, inc=1, device_id=owner_id(q)[1], device_id_type=MESH)

    fill_tables(loads, basis_v, basis_u, taps_v, taps_u, vtab, utab, sh, sw)
    for load in loads[2:]:
        load.wait()
    pl.semaphore_wait(barrier, tiles - 1 + owners - 1)

    bilinear = bilinear_of(sh, sw)
    width = send_m.shape[2]
    lane = lax.broadcasted_iota(jnp.int32, (1, width), 1)
    chunk = largest_divisor(nb, 7)
    exposure_ids = lax.broadcasted_iota(jnp.int32, coef.shape, 1)

    def data_copy(step):
        return pltpu.make_async_remote_copy(
            src_ref=send_x.at[step], dst_ref=recv_x.at[step],
            send_sem=sx_sem.at[step], recv_sem=rx_sem.at[step],
            device_id={"tile": paired(me, step, tiles)}, device_id_type=MESH,
        )

    def place_copy(step):
        return pltpu.make_async_remote_copy(
            src_ref=send_m.at[step], dst_ref=recv_m.at[step],
            send_sem=sm_sem.at[step], recv_sem=rm_sem.at[step],
            device_id={"tile": paired(me, step, tiles)}, device_id_type=MESH,
        )

    def produce(step):
        dst = paired(me, step, tiles)
        picks, live = listed_stamps(tile_dest, dst, count, cap)
        images = jnp.concatenate([stamps[p] for p in picks], axis=1)
        weights = [
            jnp.sum(jnp.where(exposure_ids == coef_index[p], coef[...], 0.0), axis=1, keepdims=True)
            for p in picks
        ]
        for base in range(0, nb, chunk):
            part = jnp.dot(
                vtab[base * sh : (base + chunk) * sh, :], images, preferred_element_type=jnp.float32
            )
            for k in range(chunk):
                for r in range(cap):
                    block = part[k * sh : (k + 1) * sh, r * sw : (r + 1) * sw]
                    scale = weights[r][base + k : base + k + 1, :]
                    tmat[r * sh : (r + 1) * sh, (base + k) * sw : (base + k + 1) * sw] = (
                        block * scale
                    ).astype(jnp.bfloat16)
        matched = jnp.dot(tmat[...], utab[...], preferred_element_type=jnp.float32)
        matched = matched.astype(jnp.bfloat16).astype(jnp.float32)
        place = jnp.full((1, width), -1, jnp.int32)
        for r in range(cap):
            p = picks[r]
            frac_rows = sub_pixel[0, p].astype(jnp.float32) * (1.0 / SUBSTEPS)
            frac_cols = sub_pixel[1, p].astype(jnp.float32) * (1.0 / SUBSTEPS)
            warped = bilinear(matched[r * sh : (r + 1) * sh, :], frac_rows, frac_cols)
            spread = bilinear(variance[p].astype(jnp.float32), frac_rows, frac_cols)
            weight = 1.0 / spread
            send_x[step, r * sh : (r + 1) * sh, 0:sw] = (weight * warped).astype(jnp.bfloat16)
            send_x[step, r * sh : (r + 1) * sh, sw : 2 * sw] = weight.astype(jnp.bfloat16)
            first = jnp.where(live[r], row_offset[p], -4 * TILE_ROWS)
            inside = (lane >= r * sh) & (lane < (r + 1) * sh)
            place = jnp.where(inside, first + lane - r * sh, place)
        send_m[step] = place

    def send_one(i, carry):
        step = tiles - 1 - i
        produce(step)
        data_copy(step).start()
        place_copy(step).start()
        return carry

    lax.fori_loop(0, tiles - 1, send_one, 0)
    produce(0)

    row_ids = lax.broadcasted_iota(jnp.int32, (TILE_ROWS, cap * sh), 0)

    def landed(block, place):
        picks = jnp.where(row_ids == place[:, : cap * sh], 1.0, 0.0).astype(jnp.bfloat16)
        return jnp.dot(picks, block, preferred_element_type=jnp.float32)

    acc[...] = landed(send_x[0], send_m[0])

    def take_one(i, carry):
        step = jnp.where(i < tiles // 2, i, tiles - 1 - (i - tiles // 2))
        data_copy(step).wait_recv()
        place_copy(step).wait_recv()
        acc[...] += landed(recv_x[step], recv_m[step])
        return carry

    lax.fori_loop(1, tiles, take_one, 0)

    def part_copy(q):
        return pltpu.make_async_remote_copy(
            src_ref=part_s.at[q], dst_ref=part_r.at[q],
            send_sem=sp_sem.at[q], recv_sem=rp_sem.at[q],
            device_id=owner_id(q)[1], device_id_type=MESH,
        )

    for q in range(1, owners):
        peer = owner_id(q)[0]
        start = pl.multiple_of(peer * own_rows, own_rows)
        part_s[q] = acc[pl.ds(start, own_rows), :].astype(jnp.bfloat16)
        part_copy(q).start()
    start = pl.multiple_of(mine * own_rows, own_rows)
    total = acc[pl.ds(start, own_rows), :]
    for q in range(1, owners):
        part_copy(q).wait_recv()
        total = total + part_r[q].astype(jnp.float32)
    out[...] = total[:, :sw] / (total[:, sw:] + 1.0)

    def drain(step, carry):
        data_copy(step).wait_send()
        place_copy(step).wait_send()
        return carry

    lax.fori_loop(1, tiles, drain, 0)
    for q in range(1, owners):
        part_copy(q).wait_send()


def paired_kernel(
    sizes,
    stamps_h, variance_h, basis_v_h, basis_u_h, coef_h, index_h, dest_h, offset_h, pixel_h,
    out,
    stamps, variance, basis_v, basis_u, coef, coef_index, tile_dest, row_offset, sub_pixel,
    taps_v, taps_u, vtab, utab, tmat, send_x, send_m, recv_x, recv_m, sum_s, sum_r, acc,
    part_s, part_r,
    in_sem, sx_sem, rx_sem, sm_sem, rm_sem, ss_sem, rs_sem, sp_sem, rp_sem,
):
    tiles, cap = sizes
    count, sh, sw = stamps.shape
    nb, tap_count = basis_v.shape
    half = (tap_count - 1) // 2
    pairs = tiles // 2
    own_rows = TILE_ROWS // 2
    rows = cap * sh
    me = lax.axis_index("tile")
    side = lax.axis_index("row") + lax.axis_index("band")
    group, core = lax.div(me, 2), lax.rem(me, 2)
    row_many = lax.axis_size("row") == 2

    def position(dx, dc):
        other = lax.rem(side + dx, 2)
        spot = {"tile": group * 2 + lax.rem(core + dc, 2)}
        spot["row" if row_many else "band"] = other
        return spot

    def far(step):
        return {"tile": paired(group, step, pairs) * 2 + core}

    loads = start_loads(
        in_sem,
        (basis_v_h, basis_v), (basis_u_h, basis_u), (stamps_h, stamps), (coef_h, coef),
        (dest_h, tile_dest), (index_h, coef_index), (offset_h, row_offset),
        (pixel_h, sub_pixel), (variance_h, variance),
    )
    slots = [(dx, dc) for dx in range(2) for dc in range(2)]
    barrier = pltpu.get_barrier_semaphore()
    for dx, dc in slots[1:]:
        pl.semaphore_signal(barrier, inc=1, device_id=position(dx, dc), device_id_type=MESH)
    for step in range(1, pairs):
        pl.semaphore_signal(barrier, inc=1, device_id=far(step), device_id_type=MESH)

    fill_tables(loads, basis_v, basis_u, taps_v, taps_u, vtab, utab, sh, sw)
    for load in loads[2:]:
        load.wait()

    width = send_m.shape[3]
    lane = lax.broadcasted_iota(jnp.int32, (1, width), 1)
    chunk = largest_divisor(nb, 7)
    exposure_ids = lax.broadcasted_iota(jnp.int32, coef.shape, 1)
    bilinear = bilinear_of(sh, sw)

    def group_copy(step, q):
        return pltpu.make_async_remote_copy(
            src_ref=send_x.at[step, q], dst_ref=recv_x.at[step, q],
            send_sem=sx_sem.at[step, q], recv_sem=rx_sem.at[step, q],
            device_id=position(*slots[q]), device_id_type=MESH,
        )

    def place_copy(step, q):
        return pltpu.make_async_remote_copy(
            src_ref=send_m.at[step, slots[q][1]], dst_ref=recv_m.at[step, q],
            send_sem=sm_sem.at[step, q], recv_sem=rm_sem.at[step, q],
            device_id=position(*slots[q]), device_id_type=MESH,
        )

    def sum_copy(step):
        return pltpu.make_async_remote_copy(
            src_ref=sum_s.at[step], dst_ref=sum_r.at[step],
            send_sem=ss_sem.at[step], recv_sem=rs_sem.at[step],
            device_id=far(step), device_id_type=MESH,
        )

    def produce(step):
        base_tile = paired(group, step, pairs) * 2
        picks, live = [], []
        for dc in range(2):
            more, alive = listed_stamps(tile_dest, base_tile + lax.rem(core + dc, 2), count, cap)
            picks += more
            live += alive
        images = jnp.concatenate([stamps[p] for p in picks], axis=1)
        weights = [
            jnp.sum(jnp.where(exposure_ids == coef_index[p], coef[...], 0.0), axis=1, keepdims=True)
            for p in picks
        ]
        for base in range(0, nb, chunk):
            part = jnp.dot(
                vtab[base * sh : (base + chunk) * sh, :], images, preferred_element_type=jnp.float32
            )
            for k in range(chunk):
                for r in range(2 * cap):
                    block = part[k * sh : (k + 1) * sh, r * sw : (r + 1) * sw]
                    tmat[r * sh : (r + 1) * sh, (base + k) * sw : (base + k + 1) * sw] = (
                        block * weights[r][base + k : base + k + 1, :]
                    ).astype(jnp.bfloat16)
        matched = jnp.dot(tmat[...], utab[...], preferred_element_type=jnp.float32)
        matched = matched.astype(jnp.bfloat16).astype(jnp.float32)
        for dc in range(2):
            place = jnp.full((1, width), -1, jnp.int32)
            for r in range(cap):
                slot = dc * cap + r
                p = picks[slot]
                frac_rows = sub_pixel[0, p].astype(jnp.float32) * (1.0 / SUBSTEPS)
                frac_cols = sub_pixel[1, p].astype(jnp.float32) * (1.0 / SUBSTEPS)
                warped = bilinear(matched[slot * sh : (slot + 1) * sh, :], frac_rows, frac_cols)
                spread = bilinear(variance[p].astype(jnp.float32), frac_rows, frac_cols)
                weight = 1.0 / spread
                numer = weight * warped
                here = jnp.where(side == 0, numer, weight).astype(jnp.bfloat16)
                there = jnp.where(side == 0, weight, numer).astype(jnp.bfloat16)
                if dc == 0:
                    recv_x[step, 0, r * sh : (r + 1) * sh, :] = here
                else:
                    send_x[step, 1, r * sh : (r + 1) * sh, :] = here
                send_x[step, 2 + dc, r * sh : (r + 1) * sh, :] = there
                first = jnp.where(live[slot], row_offset[p], -4 * TILE_ROWS)
                inside = (lane >= r * sh) & (lane < (r + 1) * sh)
                place = jnp.where(inside, first + lane - r * sh, place)
            send_m[step, dc] = place
            if dc == 0:
                recv_m[step, 0] = place

    def send_group(step):
        for q in (2, 3, 1):
            group_copy(step, q).start()
            place_copy(step, q).start()

    row_ids = lax.broadcasted_iota(jnp.int32, (TILE_ROWS, rows), 0)

    def gathered(step):
        total = None
        for q in (0, 1, 2, 3):
            if q > 0:
                group_copy(step, q).wait_recv()
                place_copy(step, q).wait_recv()
            place = recv_m[step, q]
            hit = jnp.where(row_ids == place[:, :rows], 1.0, 0.0).astype(jnp.bfloat16)
            part = jnp.dot(hit, recv_x[step, q], preferred_element_type=jnp.float32)
            total = part if total is None else total + part
        return total

    produce(pairs - 1)
    pl.semaphore_wait(barrier, len(slots) - 1 + pairs - 1)
    send_group(pairs - 1)

    def one_step(i, carry):
        step = pairs - 1 - i
        produce(step)
        send_group(step)
        sum_s[step + 1] = gathered(step + 1).astype(jnp.bfloat16)
        sum_copy(step + 1).start()
        return carry

    lax.fori_loop(1, pairs, one_step, 0)
    acc[...] = gathered(0)
    for step in range(1, pairs):
        sum_copy(step).wait_recv()
        acc[...] += sum_r[step].astype(jnp.float32)

    part_copy = pltpu.make_async_remote_copy(
        src_ref=part_s, dst_ref=part_r, send_sem=sp_sem.at[0], recv_sem=rp_sem.at[0],
        device_id=position(1, 0), device_id_type=MESH,
    )
    start = pl.multiple_of((1 - side) * own_rows, own_rows)
    part_s[...] = acc[pl.ds(start, own_rows), :].astype(jnp.bfloat16)
    part_copy.start()
    own = acc[pl.ds(pl.multiple_of(side * own_rows, own_rows), own_rows), :]
    part_copy.wait_recv()
    other = part_r[...].astype(jnp.float32)
    out[...] = jnp.where(side == 0, own, other) / (jnp.where(side == 0, other, own) + 1.0)

    def drain(step, carry):
        for q in (1, 2, 3):
            group_copy(step, q).wait_send()
            place_copy(step, q).wait_send()
        return carry

    lax.fori_loop(0, pairs, drain, 0)
    for step in range(1, pairs):
        sum_copy(step).wait_send()
    part_copy.wait_send()


def local(
    stamps, variance, basis_v, basis_u, coefficients, coef_index, tile_dest, row_offset, sub_pixel
):
    tiles = lax.axis_size("tile")
    rows_n = lax.axis_size("row")
    bands = lax.axis_size("band")
    count, sh, sw = stamps.shape
    nb = basis_v.shape[0]
    cap = max(2, (count + tiles - 1) // tiles)
    owners = rows_n * bands
    own_rows = TILE_ROWS // owners
    width = -(-cap * sh // 128) * 128
    vmem = pl.BlockSpec(memory_space=pltpu.VMEM)
    anywhere = pl.BlockSpec(memory_space=pl.ANY)
    coefficients, sub_pixel = coefficients.T, sub_pixel.T
    big = [stamps, variance, basis_v, basis_u, coefficients]
    small = [coef_index, tile_dest, row_offset, sub_pixel]
    bf16, f32, dma = jnp.bfloat16, jnp.float32, pltpu.SemaphoreType.DMA
    inputs = [
        *(pltpu.VMEM(x.shape, x.dtype) for x in big),
        *(pltpu.SMEM(x.shape, x.dtype) for x in small),
        pltpu.VMEM((nb, sw), f32),
        pltpu.VMEM((nb, sw), f32),
        pltpu.VMEM((nb * sh, sh), bf16),
        pltpu.VMEM((nb * sw, sw), bf16),
    ]
    params = pltpu.CompilerParams(
        collective_id=0, has_side_effects=True, vmem_limit_bytes=56 * 1024 * 1024
    )
    if owners == 2 and tiles % 2 == 0 and tiles > 2:
        pairs = tiles // 2
        return pl.pallas_call(
            functools.partial(paired_kernel, (tiles, cap)),
            out_shape=jax.ShapeDtypeStruct((own_rows, sw), f32),
            in_specs=[anywhere] * 9,
            out_specs=vmem,
            scratch_shapes=[
                *inputs,
                pltpu.VMEM((2 * cap * sh, nb * sw), bf16),
                pltpu.VMEM((pairs, 4, cap * sh, sw), bf16),
                pltpu.VMEM((pairs, 2, 1, width), jnp.int32),
                pltpu.VMEM((pairs, 4, cap * sh, sw), bf16),
                pltpu.VMEM((pairs, 4, 1, width), jnp.int32),
                pltpu.VMEM((pairs, TILE_ROWS, sw), bf16),
                pltpu.VMEM((pairs, TILE_ROWS, sw), bf16),
                pltpu.VMEM((TILE_ROWS, sw), f32),
                pltpu.VMEM((own_rows, sw), bf16),
                pltpu.VMEM((own_rows, sw), bf16),
                dma((9,)),
                *(dma((pairs, 4)) for _ in range(4)),
                dma((pairs,)),
                dma((pairs,)),
                dma((1,)),
                dma((1,)),
            ],
            compiler_params=params,
        )(*big, *small)
    return pl.pallas_call(
        functools.partial(kernel, (tiles, rows_n, bands, cap)),
        out_shape=jax.ShapeDtypeStruct((own_rows, sw), f32),
        in_specs=[anywhere] * 9,
        out_specs=vmem,
        scratch_shapes=[
            *inputs,
            pltpu.VMEM((cap * sh, nb * sw), bf16),
            pltpu.VMEM((tiles, cap * sh, 2 * sw), bf16),
            pltpu.VMEM((tiles, 1, width), jnp.int32),
            pltpu.VMEM((tiles, cap * sh, 2 * sw), bf16),
            pltpu.VMEM((tiles, 1, width), jnp.int32),
            pltpu.VMEM((TILE_ROWS, 2 * sw), f32),
            pltpu.VMEM((owners, own_rows, 2 * sw), bf16),
            pltpu.VMEM((owners, own_rows, 2 * sw), bf16),
            pltpu.SemaphoreType.DMA((9,)),
            pltpu.SemaphoreType.DMA((tiles,)),
            pltpu.SemaphoreType.DMA((tiles,)),
            pltpu.SemaphoreType.DMA((tiles,)),
            pltpu.SemaphoreType.DMA((tiles,)),
            pltpu.SemaphoreType.DMA((owners,)),
            pltpu.SemaphoreType.DMA((owners,)),
        ],
        compiler_params=params,
    )(*big, *small)


def solution(mesh):
    in_specs = (
        P(("patch", "tile", "row", "band"), None, None),
        P(("patch", "tile", "row", "band"), None, None),
        P(),
        P(),
        P("patch", None),
        P(("patch", "tile", "row", "band")),
        P(("patch", "tile", "row", "band")),
        P(("patch", "tile", "row", "band")),
        P(("patch", "tile", "row", "band"), None),
    )
    out_specs = P(("patch", "tile", "row", "band"), None)
    return jax.shard_map(local, mesh=mesh, in_specs=in_specs, out_specs=out_specs, check_vma=False)
```

```python
import functools

import jax
import jax.numpy as jnp
from jax import lax
from jax.experimental import pallas as pl
from jax.experimental.pallas import tpu as pltpu
from jax.sharding import PartitionSpec as P

SUBSTEPS = 64
TILE_ROWS = 512
MESH = pl.DeviceIdType.MESH


def largest_divisor(value, limit):
    return max(d for d in range(1, limit + 1) if value % d == 0)


def paired(index, step, count):
    if count & (count - 1):
        return lax.rem(index + step, count)
    total, bit = 0, 1
    while bit < count:
        digit = lax.rem(lax.div(index, bit), 2) + lax.rem(lax.div(step, bit), 2)
        total = total + lax.rem(digit, 2) * bit
        bit *= 2
    return total


def start_loads(sems, *pairs):
    loads = [pltpu.make_async_copy(src, dst, sems.at[i]) for i, (src, dst) in enumerate(pairs)]
    for load in loads:
        load.start()
    return loads


def bilinear_of(sh, sw):
    last_row = lax.broadcasted_iota(jnp.int32, (sh, sw), 0) == sh - 1
    last_col = lax.broadcasted_iota(jnp.int32, (sh, sw), 1) == sw - 1

    def bilinear(values, frac_rows, frac_cols):
        below = jnp.where(last_row, values, pltpu.roll(values, sh - 1, 0))
        mixed = (1.0 - frac_rows) * values + frac_rows * below
        beside = jnp.where(last_col, mixed, pltpu.roll(mixed, sw - 1, 1))
        return (1.0 - frac_cols) * mixed + frac_cols * beside

    return bilinear


def listed_stamps(tile_dest, dst, count, cap):
    bits = count.bit_length()
    listed = jnp.int32(0)
    for s in range(count):
        listed = jnp.where(tile_dest[s] == dst, (listed << bits) + (s + 1), listed)
    picks, live = [], []
    for r in range(cap):
        digit = listed & ((1 << bits) - 1)
        listed = listed >> bits
        picks.append(jnp.maximum(digit - 1, 0))
        live.append(digit > 0)
    return picks, live


def fill_tables(loads, basis_v, basis_u, taps_v, taps_u, vtab, utab, sh, sw):
    nb, tap_count = basis_v.shape
    half = (tap_count - 1) // 2
    tap_ids = lax.broadcasted_iota(jnp.int32, (tap_count, sw), 0)
    lag_ids = lax.broadcasted_iota(jnp.int32, (tap_count, sw), 1)
    lag_ids = jnp.where(lag_ids > half, lag_ids - sw, lag_ids)
    forward = jnp.where(tap_ids == lag_ids + half, 1.0, 0.0).astype(jnp.bfloat16)
    mirrored = jnp.where(tap_ids == half - lag_ids, 1.0, 0.0).astype(jnp.bfloat16)
    loads[0].wait()
    taps_v[...] = jnp.dot(basis_v[...], forward, preferred_element_type=jnp.float32)
    loads[1].wait()
    taps_u[...] = jnp.dot(basis_u[...], mirrored, preferred_element_type=jnp.float32)
    lag = lax.broadcasted_iota(jnp.int32, (sw, sw), 1) - lax.broadcasted_iota(jnp.int32, (sw, sw), 0)
    near = jnp.abs(lag) <= half
    for k in range(nb):
        line = jnp.broadcast_to(taps_v[k : k + 1, :], (sh, sw))
        rolled = pltpu.roll(line, 0, 1, stride=1, stride_axis=0)
        vtab[k * sh : (k + 1) * sh, :] = rolled[:, :sh].astype(jnp.bfloat16)
        line = jnp.broadcast_to(taps_u[k : k + 1, :], (sw, sw))
        rolled = pltpu.roll(line, 0, 1, stride=1, stride_axis=0)
        utab[k * sw : (k + 1) * sw, :] = jnp.where(near, rolled, 0.0).astype(jnp.bfloat16)


def kernel(
    sizes,
    stamps_h, variance_h, basis_v_h, basis_u_h, coef_h, index_h, dest_h, offset_h, pixel_h,
    out,
    stamps, variance, basis_v, basis_u, coef, coef_index, tile_dest, row_offset, sub_pixel,
    taps_v, taps_u, vtab, utab, tmat, send_x, send_m, recv_x, recv_m, acc, part_s, part_r,
    in_sem, sx_sem, rx_sem, sm_sem, rm_sem, sp_sem, rp_sem,
):
    loads = start_loads(
        in_sem,
        (basis_v_h, basis_v), (basis_u_h, basis_u), (stamps_h, stamps), (coef_h, coef),
        (dest_h, tile_dest), (index_h, coef_index), (offset_h, row_offset),
        (pixel_h, sub_pixel), (variance_h, variance),
    )
    tiles, rows_n, bands, cap = sizes
    count, sh, sw = stamps.shape
    nb, tap_count = basis_v.shape
    half = (tap_count - 1) // 2
    owners = rows_n * bands
    own_rows = TILE_ROWS // owners
    me = lax.axis_index("tile")
    mine = lax.axis_index("row") * bands + lax.axis_index("band")

    def owner_id(q):
        peer = lax.rem(mine + q, owners)
        return peer, {"row": lax.div(peer, bands), "band": lax.rem(peer, bands)}

    barrier = pltpu.get_barrier_semaphore()
    for step in range(1, tiles):
        pl.semaphore_signal(
            barrier, inc=1, device_id={"tile": lax.rem(me + step, tiles)}, device_id_type=MESH
        )
    for q in range(1, owners):
        pl.semaphore_signal(barrier, inc=1, device_id=owner_id(q)[1], device_id_type=MESH)

    fill_tables(loads, basis_v, basis_u, taps_v, taps_u, vtab, utab, sh, sw)
    for load in loads[2:]:
        load.wait()
    pl.semaphore_wait(barrier, tiles - 1 + owners - 1)

    bilinear = bilinear_of(sh, sw)
    width = send_m.shape[2]
    lane = lax.broadcasted_iota(jnp.int32, (1, width), 1)
    chunk = largest_divisor(nb, 7)
    exposure_ids = lax.broadcasted_iota(jnp.int32, coef.shape, 1)

    def data_copy(step):
        return pltpu.make_async_remote_copy(
            src_ref=send_x.at[step], dst_ref=recv_x.at[step],
            send_sem=sx_sem.at[step], recv_sem=rx_sem.at[step],
            device_id={"tile": paired(me, step, tiles)}, device_id_type=MESH,
        )

    def place_copy(step):
        return pltpu.make_async_remote_copy(
            src_ref=send_m.at[step], dst_ref=recv_m.at[step],
            send_sem=sm_sem.at[step], recv_sem=rm_sem.at[step],
            device_id={"tile": paired(me, step, tiles)}, device_id_type=MESH,
        )

    def produce(step):
        dst = paired(me, step, tiles)
        picks, live = listed_stamps(tile_dest, dst, count, cap)
        images = jnp.concatenate([stamps[p] for p in picks], axis=1)
        weights = [
            jnp.sum(jnp.where(exposure_ids == coef_index[p], coef[...], 0.0), axis=1, keepdims=True)
            for p in picks
        ]
        for base in range(0, nb, chunk):
            part = jnp.dot(
                vtab[base * sh : (base + chunk) * sh, :], images, preferred_element_type=jnp.float32
            )
            for k in range(chunk):
                for r in range(cap):
                    block = part[k * sh : (k + 1) * sh, r * sw : (r + 1) * sw]
                    scale = weights[r][base + k : base + k + 1, :]
                    tmat[r * sh : (r + 1) * sh, (base + k) * sw : (base + k + 1) * sw] = (
                        block * scale
                    ).astype(jnp.bfloat16)
        matched = jnp.dot(tmat[...], utab[...], preferred_element_type=jnp.float32)
        matched = matched.astype(jnp.bfloat16).astype(jnp.float32)
        place = jnp.full((1, width), -1, jnp.int32)
        for r in range(cap):
            p = picks[r]
            frac_rows = sub_pixel[0, p].astype(jnp.float32) * (1.0 / SUBSTEPS)
            frac_cols = sub_pixel[1, p].astype(jnp.float32) * (1.0 / SUBSTEPS)
            warped = bilinear(matched[r * sh : (r + 1) * sh, :], frac_rows, frac_cols)
            spread = bilinear(variance[p].astype(jnp.float32), frac_rows, frac_cols)
            weight = 1.0 / spread
            send_x[step, r * sh : (r + 1) * sh, 0:sw] = (weight * warped).astype(jnp.bfloat16)
            send_x[step, r * sh : (r + 1) * sh, sw : 2 * sw] = weight.astype(jnp.bfloat16)
            first = jnp.where(live[r], row_offset[p], -4 * TILE_ROWS)
            inside = (lane >= r * sh) & (lane < (r + 1) * sh)
            place = jnp.where(inside, first + lane - r * sh, place)
        send_m[step] = place

    def send_one(i, carry):
        step = tiles - 1 - i
        produce(step)
        data_copy(step).start()
        place_copy(step).start()
        return carry

    lax.fori_loop(0, tiles - 1, send_one, 0)
    produce(0)

    row_ids = lax.broadcasted_iota(jnp.int32, (TILE_ROWS, cap * sh), 0)

    def landed(block, place):
        picks = jnp.where(row_ids == place[:, : cap * sh], 1.0, 0.0).astype(jnp.bfloat16)
        return jnp.dot(picks, block, preferred_element_type=jnp.float32)

    acc[...] = landed(send_x[0], send_m[0])

    def take_one(i, carry):
        step = jnp.where(i < tiles // 2, i, tiles - 1 - (i - tiles // 2))
        data_copy(step).wait_recv()
        place_copy(step).wait_recv()
        acc[...] += landed(recv_x[step], recv_m[step])
        return carry

    lax.fori_loop(1, tiles, take_one, 0)

    def part_copy(q):
        return pltpu.make_async_remote_copy(
            src_ref=part_s.at[q], dst_ref=part_r.at[q],
            send_sem=sp_sem.at[q], recv_sem=rp_sem.at[q],
            device_id=owner_id(q)[1], device_id_type=MESH,
        )

    for q in range(1, owners):
        peer = owner_id(q)[0]
        start = pl.multiple_of(peer * own_rows, own_rows)
        part_s[q] = acc[pl.ds(start, own_rows), :].astype(jnp.bfloat16)
        part_copy(q).start()
    start = pl.multiple_of(mine * own_rows, own_rows)
    total = acc[pl.ds(start, own_rows), :]
    for q in range(1, owners):
        part_copy(q).wait_recv()
        total = total + part_r[q].astype(jnp.float32)
    out[...] = total[:, :sw] / (total[:, sw:] + 1.0)

    def drain(step, carry):
        data_copy(step).wait_send()
        place_copy(step).wait_send()
        return carry

    lax.fori_loop(1, tiles, drain, 0)
    for q in range(1, owners):
        part_copy(q).wait_send()


def paired_kernel(
    sizes,
    stamps_h, variance_h, basis_v_h, basis_u_h, coef_h, index_h, dest_h, offset_h, pixel_h,
    out,
    stamps, variance, basis_v, basis_u, coef, coef_index, tile_dest, row_offset, sub_pixel,
    taps_v, taps_u, vtab, utab, tmat, send_x, send_m, recv_x, recv_m, sum_s, sum_r, acc,
    part_s, part_r,
    in_sem, sx_sem, rx_sem, sm_sem, rm_sem, ss_sem, rs_sem, sp_sem, rp_sem,
):
    tiles, cap = sizes
    count, sh, sw = stamps.shape
    nb, tap_count = basis_v.shape
    half = (tap_count - 1) // 2
    pairs = tiles // 2
    own_rows = TILE_ROWS // 2
    rows = cap * sh
    me = lax.axis_index("tile")
    side = lax.axis_index("row") + lax.axis_index("band")
    group, core = lax.div(me, 2), lax.rem(me, 2)
    row_many = lax.axis_size("row") == 2

    def position(dx, dc):
        other = lax.rem(side + dx, 2)
        spot = {"tile": group * 2 + lax.rem(core + dc, 2)}
        spot["row" if row_many else "band"] = other
        return spot

    def far(step):
        return {"tile": paired(group, step, pairs) * 2 + core}

    loads = start_loads(
        in_sem,
        (basis_v_h, basis_v), (basis_u_h, basis_u), (stamps_h, stamps), (coef_h, coef),
        (dest_h, tile_dest), (index_h, coef_index), (offset_h, row_offset),
        (pixel_h, sub_pixel), (variance_h, variance),
    )
    slots = [(dx, dc) for dx in range(2) for dc in range(2)]
    barrier = pltpu.get_barrier_semaphore()
    for dx, dc in slots[1:]:
        pl.semaphore_signal(barrier, inc=1, device_id=position(dx, dc), device_id_type=MESH)
    for step in range(1, pairs):
        pl.semaphore_signal(barrier, inc=1, device_id=far(step), device_id_type=MESH)

    fill_tables(loads, basis_v, basis_u, taps_v, taps_u, vtab, utab, sh, sw)
    for load in loads[2:]:
        load.wait()

    width = send_m.shape[3]
    lane = lax.broadcasted_iota(jnp.int32, (1, width), 1)
    chunk = largest_divisor(nb, 3)
    exposure_ids = lax.broadcasted_iota(jnp.int32, coef.shape, 1)
    bilinear = bilinear_of(sh, sw)

    def group_copy(step, q):
        return pltpu.make_async_remote_copy(
            src_ref=send_x.at[step, q], dst_ref=recv_x.at[step, q],
            send_sem=sx_sem.at[step, q], recv_sem=rx_sem.at[step, q],
            device_id=position(*slots[q]), device_id_type=MESH,
        )

    def place_copy(step, q):
        return pltpu.make_async_remote_copy(
            src_ref=send_m.at[step, slots[q][1]], dst_ref=recv_m.at[step, q],
            send_sem=sm_sem.at[step, q], recv_sem=rm_sem.at[step, q],
            device_id=position(*slots[q]), device_id_type=MESH,
        )

    def sum_copy(step):
        return pltpu.make_async_remote_copy(
            src_ref=sum_s.at[step], dst_ref=sum_r.at[step],
            send_sem=ss_sem.at[step], recv_sem=rs_sem.at[step],
            device_id=far(step), device_id_type=MESH,
        )

    def produce(step):
        base_tile = paired(group, step, pairs) * 2
        picks, live = [], []
        for dc in range(2):
            more, alive = listed_stamps(tile_dest, base_tile + lax.rem(core + dc, 2), count, cap)
            picks += more
            live += alive
        images = jnp.concatenate([stamps[p] for p in picks], axis=1)
        weights = [
            jnp.sum(jnp.where(exposure_ids == coef_index[p], coef[...], 0.0), axis=1, keepdims=True)
            for p in picks
        ]
        def across(first, last):
            return jnp.dot(
                tmat[:, first * sw : last * sw],
                utab[first * sw : last * sw, :],
                preferred_element_type=jnp.float32,
            )

        matched, done = None, 0
        for base in range(0, nb, chunk):
            ready = base - base % (2 * chunk)
            part = jnp.dot(
                vtab[base * sh : (base + chunk) * sh, :], images, preferred_element_type=jnp.float32
            )
            for k in range(chunk):
                for r in range(2 * cap):
                    block = part[k * sh : (k + 1) * sh, r * sw : (r + 1) * sw]
                    tmat[r * sh : (r + 1) * sh, (base + k) * sw : (base + k + 1) * sw] = (
                        block * weights[r][base + k : base + k + 1, :]
                    ).astype(jnp.bfloat16)
            if ready > done:
                term = across(done, ready)
                matched = term if matched is None else matched + term
                done = ready
        term = across(done, nb)
        matched = term if matched is None else matched + term
        matched = matched.astype(jnp.bfloat16).astype(jnp.float32)
        for dc in range(2):
            place = jnp.full((1, width), -4 * TILE_ROWS, jnp.int32)
            for r in range(cap):
                slot = dc * cap + r
                p = picks[slot]
                frac_rows = sub_pixel[0, p].astype(jnp.float32) * (1.0 / SUBSTEPS)
                frac_cols = sub_pixel[1, p].astype(jnp.float32) * (1.0 / SUBSTEPS)
                warped = bilinear(matched[slot * sh : (slot + 1) * sh, :], frac_rows, frac_cols)
                spread = bilinear(variance[p].astype(jnp.float32), frac_rows, frac_cols)
                weight = 1.0 / spread
                numer = weight * warped
                here = jnp.where(side == 0, numer, weight).astype(jnp.bfloat16)
                there = jnp.where(side == 0, weight, numer).astype(jnp.bfloat16)
                if dc == 0:
                    recv_x[step, 0, r * sh : (r + 1) * sh, :] = here
                else:
                    send_x[step, 1, r * sh : (r + 1) * sh, :] = here
                send_x[step, 2 + dc, r * sh : (r + 1) * sh, :] = there
                first = jnp.where(live[slot], row_offset[p], -4 * TILE_ROWS)
                inside = (lane >= r * sh) & (lane < (r + 1) * sh)
                place = jnp.where(inside, first + lane - r * sh, place)
            send_m[step, dc] = place
            if dc == 0:
                recv_m[step, 0] = place

    def send_group(step):
        for q in (2, 3, 1):
            group_copy(step, q).start()
            place_copy(step, q).start()

    middle = TILE_ROWS // 2
    row_ids = lax.broadcasted_iota(jnp.int32, (TILE_ROWS, rows), 0) - middle
    row_ids = row_ids.astype(jnp.float32).astype(jnp.bfloat16)
    one, zero = jnp.bfloat16(1.0), jnp.bfloat16(0.0)

    def gathered(step):
        total = None
        for q in (0, 1, 2, 3):
            if q > 0:
                group_copy(step, q).wait_recv()
                place_copy(step, q).wait_recv()
            place = (recv_m[step, q] - middle).astype(jnp.float32).astype(jnp.bfloat16)
            hit = jnp.where(row_ids == place[:, :rows], one, zero)
            part = jnp.dot(hit, recv_x[step, q], preferred_element_type=jnp.float32)
            total = part if total is None else total + part
        return total

    produce(pairs - 1)
    pl.semaphore_wait(barrier, len(slots) - 1 + pairs - 1)
    send_group(pairs - 1)

    def one_step(i, carry):
        step = pairs - 1 - i
        produce(step)
        send_group(step)
        sum_s[step + 1] = gathered(step + 1).astype(jnp.bfloat16)
        sum_copy(step + 1).start()
        return carry

    lax.fori_loop(1, pairs, one_step, 0)
    acc[...] = gathered(0)
    for step in range(1, pairs):
        sum_copy(step).wait_recv()
        acc[...] += sum_r[step].astype(jnp.float32)

    part_copy = pltpu.make_async_remote_copy(
        src_ref=part_s, dst_ref=part_r, send_sem=sp_sem.at[0], recv_sem=rp_sem.at[0],
        device_id=position(1, 0), device_id_type=MESH,
    )
    start = pl.multiple_of((1 - side) * own_rows, own_rows)
    part_s[...] = acc[pl.ds(start, own_rows), :].astype(jnp.bfloat16)
    part_copy.start()
    own = acc[pl.ds(pl.multiple_of(side * own_rows, own_rows), own_rows), :]
    part_copy.wait_recv()
    other = part_r[...].astype(jnp.float32)
    out[...] = jnp.where(side == 0, own, other) / (jnp.where(side == 0, other, own) + 1.0)

    def drain(step, carry):
        for q in (1, 2, 3):
            group_copy(step, q).wait_send()
            place_copy(step, q).wait_send()
        return carry

    lax.fori_loop(0, pairs, drain, 0)
    for step in range(1, pairs):
        sum_copy(step).wait_send()
    part_copy.wait_send()


def local(
    stamps, variance, basis_v, basis_u, coefficients, coef_index, tile_dest, row_offset, sub_pixel
):
    tiles = lax.axis_size("tile")
    rows_n = lax.axis_size("row")
    bands = lax.axis_size("band")
    count, sh, sw = stamps.shape
    nb = basis_v.shape[0]
    cap = max(2, (count + tiles - 1) // tiles)
    owners = rows_n * bands
    own_rows = TILE_ROWS // owners
    width = -(-cap * sh // 128) * 128
    vmem = pl.BlockSpec(memory_space=pltpu.VMEM)
    anywhere = pl.BlockSpec(memory_space=pl.ANY)
    coefficients, sub_pixel = coefficients.T, sub_pixel.T
    big = [stamps, variance, basis_v, basis_u, coefficients]
    small = [coef_index, tile_dest, row_offset, sub_pixel]
    bf16, f32, dma = jnp.bfloat16, jnp.float32, pltpu.SemaphoreType.DMA
    inputs = [
        *(pltpu.VMEM(x.shape, x.dtype) for x in big),
        *(pltpu.SMEM(x.shape, x.dtype) for x in small),
        pltpu.VMEM((nb, sw), f32),
        pltpu.VMEM((nb, sw), f32),
        pltpu.VMEM((nb * sh, sh), bf16),
        pltpu.VMEM((nb * sw, sw), bf16),
    ]
    params = pltpu.CompilerParams(
        collective_id=0, has_side_effects=True, vmem_limit_bytes=56 * 1024 * 1024
    )
    if owners == 2 and tiles % 2 == 0 and tiles > 2:
        pairs = tiles // 2
        return pl.pallas_call(
            functools.partial(paired_kernel, (tiles, cap)),
            out_shape=jax.ShapeDtypeStruct((own_rows, sw), f32),
            in_specs=[anywhere] * 9,
            out_specs=vmem,
            scratch_shapes=[
                *inputs,
                pltpu.VMEM((2 * cap * sh, nb * sw), bf16),
                pltpu.VMEM((pairs, 4, cap * sh, sw), bf16),
                pltpu.VMEM((pairs, 2, 1, width), jnp.int32),
                pltpu.VMEM((pairs, 4, cap * sh, sw), bf16),
                pltpu.VMEM((pairs, 4, 1, width), jnp.int32),
                pltpu.VMEM((pairs, TILE_ROWS, sw), bf16),
                pltpu.VMEM((pairs, TILE_ROWS, sw), bf16),
                pltpu.VMEM((TILE_ROWS, sw), f32),
                pltpu.VMEM((own_rows, sw), bf16),
                pltpu.VMEM((own_rows, sw), bf16),
                dma((9,)),
                *(dma((pairs, 4)) for _ in range(4)),
                dma((pairs,)),
                dma((pairs,)),
                dma((1,)),
                dma((1,)),
            ],
            compiler_params=params,
        )(*big, *small)
    return pl.pallas_call(
        functools.partial(kernel, (tiles, rows_n, bands, cap)),
        out_shape=jax.ShapeDtypeStruct((own_rows, sw), f32),
        in_specs=[anywhere] * 9,
        out_specs=vmem,
        scratch_shapes=[
            *inputs,
            pltpu.VMEM((cap * sh, nb * sw), bf16),
            pltpu.VMEM((tiles, cap * sh, 2 * sw), bf16),
            pltpu.VMEM((tiles, 1, width), jnp.int32),
            pltpu.VMEM((tiles, cap * sh, 2 * sw), bf16),
            pltpu.VMEM((tiles, 1, width), jnp.int32),
            pltpu.VMEM((TILE_ROWS, 2 * sw), f32),
            pltpu.VMEM((owners, own_rows, 2 * sw), bf16),
            pltpu.VMEM((owners, own_rows, 2 * sw), bf16),
            pltpu.SemaphoreType.DMA((9,)),
            pltpu.SemaphoreType.DMA((tiles,)),
            pltpu.SemaphoreType.DMA((tiles,)),
            pltpu.SemaphoreType.DMA((tiles,)),
            pltpu.SemaphoreType.DMA((tiles,)),
            pltpu.SemaphoreType.DMA((owners,)),
            pltpu.SemaphoreType.DMA((owners,)),
        ],
        compiler_params=params,
    )(*big, *small)


def solution(mesh):
    in_specs = (
        P(("patch", "tile", "row", "band"), None, None),
        P(("patch", "tile", "row", "band"), None, None),
        P(),
        P(),
        P("patch", None),
        P(("patch", "tile", "row", "band")),
        P(("patch", "tile", "row", "band")),
        P(("patch", "tile", "row", "band")),
        P(("patch", "tile", "row", "band"), None),
    )
    out_specs = P(("patch", "tile", "row", "band"), None)
    return jax.shard_map(local, mesh=mesh, in_specs=in_specs, out_specs=out_specs, check_vma=False)
```

```python
import functools

import jax
import jax.numpy as jnp
from jax import lax
from jax.experimental import pallas as pl
from jax.experimental.pallas import tpu as pltpu
from jax.sharding import PartitionSpec as P

SUBSTEPS = 64
TILE_ROWS = 512
MESH = pl.DeviceIdType.MESH


def largest_divisor(value, limit):
    return max(d for d in range(1, limit + 1) if value % d == 0)


def paired(index, step, count):
    if count & (count - 1):
        return lax.rem(index + step, count)
    total, bit = 0, 1
    while bit < count:
        digit = lax.rem(lax.div(index, bit), 2) + lax.rem(lax.div(step, bit), 2)
        total = total + lax.rem(digit, 2) * bit
        bit *= 2
    return total


def start_loads(sems, *pairs):
    loads = [pltpu.make_async_copy(src, dst, sems.at[i]) for i, (src, dst) in enumerate(pairs)]
    for load in loads:
        load.start()
    return loads


def bilinear_of(sh, sw):
    last_row = lax.broadcasted_iota(jnp.int32, (sh, sw), 0) == sh - 1
    last_col = lax.broadcasted_iota(jnp.int32, (sh, sw), 1) == sw - 1

    def bilinear(values, frac_rows, frac_cols):
        below = jnp.where(last_row, values, pltpu.roll(values, sh - 1, 0))
        mixed = (1.0 - frac_rows) * values + frac_rows * below
        beside = jnp.where(last_col, mixed, pltpu.roll(mixed, sw - 1, 1))
        return (1.0 - frac_cols) * mixed + frac_cols * beside

    return bilinear


def listed_stamps(tile_dest, dst, count, cap):
    bits = count.bit_length()
    listed = jnp.int32(0)
    for s in range(count):
        listed = jnp.where(tile_dest[s] == dst, (listed << bits) + (s + 1), listed)
    picks, live = [], []
    for r in range(cap):
        digit = listed & ((1 << bits) - 1)
        listed = listed >> bits
        picks.append(jnp.maximum(digit - 1, 0))
        live.append(digit > 0)
    return picks, live


def fill_tables(loads, basis_v, basis_u, taps_v, taps_u, vtab, utab, sh, sw):
    nb, tap_count = basis_v.shape
    half = (tap_count - 1) // 2
    tap_ids = lax.broadcasted_iota(jnp.int32, (tap_count, sw), 0)
    lag_ids = lax.broadcasted_iota(jnp.int32, (tap_count, sw), 1)
    lag_ids = jnp.where(lag_ids > half, lag_ids - sw, lag_ids)
    forward = jnp.where(tap_ids == lag_ids + half, 1.0, 0.0).astype(jnp.bfloat16)
    mirrored = jnp.where(tap_ids == half - lag_ids, 1.0, 0.0).astype(jnp.bfloat16)
    loads[0].wait()
    taps_v[...] = jnp.dot(basis_v[...], forward, preferred_element_type=jnp.float32)
    loads[1].wait()
    taps_u[...] = jnp.dot(basis_u[...], mirrored, preferred_element_type=jnp.float32)
    lag = lax.broadcasted_iota(jnp.int32, (sw, sw), 1) - lax.broadcasted_iota(jnp.int32, (sw, sw), 0)
    near = jnp.abs(lag) <= half
    for k in range(nb):
        line = jnp.broadcast_to(taps_v[k : k + 1, :], (sh, sw))
        rolled = pltpu.roll(line, 0, 1, stride=1, stride_axis=0)
        vtab[k * sh : (k + 1) * sh, :] = rolled[:, :sh].astype(jnp.bfloat16)
        line = jnp.broadcast_to(taps_u[k : k + 1, :], (sw, sw))
        rolled = pltpu.roll(line, 0, 1, stride=1, stride_axis=0)
        utab[k * sw : (k + 1) * sw, :] = jnp.where(near, rolled, 0.0).astype(jnp.bfloat16)


def kernel(
    sizes,
    stamps_h, variance_h, basis_v_h, basis_u_h, coef_h, index_h, dest_h, offset_h, pixel_h,
    out,
    stamps, variance, basis_v, basis_u, coef, coef_index, tile_dest, row_offset, sub_pixel,
    taps_v, taps_u, vtab, utab, tmat, send_x, send_m, recv_x, recv_m, acc, part_s, part_r,
    in_sem, sx_sem, rx_sem, sm_sem, rm_sem, sp_sem, rp_sem,
):
    loads = start_loads(
        in_sem,
        (basis_v_h, basis_v), (basis_u_h, basis_u), (stamps_h, stamps), (coef_h, coef),
        (dest_h, tile_dest), (index_h, coef_index), (offset_h, row_offset),
        (pixel_h, sub_pixel), (variance_h, variance),
    )
    tiles, rows_n, bands, cap = sizes
    count, sh, sw = stamps.shape
    nb, tap_count = basis_v.shape
    half = (tap_count - 1) // 2
    owners = rows_n * bands
    own_rows = TILE_ROWS // owners
    me = lax.axis_index("tile")
    mine = lax.axis_index("row") * bands + lax.axis_index("band")

    def owner_id(q):
        peer = lax.rem(mine + q, owners)
        return peer, {"row": lax.div(peer, bands), "band": lax.rem(peer, bands)}

    barrier = pltpu.get_barrier_semaphore()
    for step in range(1, tiles):
        pl.semaphore_signal(
            barrier, inc=1, device_id={"tile": lax.rem(me + step, tiles)}, device_id_type=MESH
        )
    for q in range(1, owners):
        pl.semaphore_signal(barrier, inc=1, device_id=owner_id(q)[1], device_id_type=MESH)

    fill_tables(loads, basis_v, basis_u, taps_v, taps_u, vtab, utab, sh, sw)
    for load in loads[2:]:
        load.wait()
    pl.semaphore_wait(barrier, tiles - 1 + owners - 1)

    bilinear = bilinear_of(sh, sw)
    width = send_m.shape[2]
    lane = lax.broadcasted_iota(jnp.int32, (1, width), 1)
    chunk = largest_divisor(nb, 7)
    exposure_ids = lax.broadcasted_iota(jnp.int32, coef.shape, 1)

    def data_copy(step):
        return pltpu.make_async_remote_copy(
            src_ref=send_x.at[step], dst_ref=recv_x.at[step],
            send_sem=sx_sem.at[step], recv_sem=rx_sem.at[step],
            device_id={"tile": paired(me, step, tiles)}, device_id_type=MESH,
        )

    def place_copy(step):
        return pltpu.make_async_remote_copy(
            src_ref=send_m.at[step], dst_ref=recv_m.at[step],
            send_sem=sm_sem.at[step], recv_sem=rm_sem.at[step],
            device_id={"tile": paired(me, step, tiles)}, device_id_type=MESH,
        )

    def produce(step):
        dst = paired(me, step, tiles)
        picks, live = listed_stamps(tile_dest, dst, count, cap)
        images = jnp.concatenate([stamps[p] for p in picks], axis=1)
        weights = [
            jnp.sum(jnp.where(exposure_ids == coef_index[p], coef[...], 0.0), axis=1, keepdims=True)
            for p in picks
        ]
        for base in range(0, nb, chunk):
            part = jnp.dot(
                vtab[base * sh : (base + chunk) * sh, :], images, preferred_element_type=jnp.float32
            )
            for k in range(chunk):
                for r in range(cap):
                    block = part[k * sh : (k + 1) * sh, r * sw : (r + 1) * sw]
                    scale = weights[r][base + k : base + k + 1, :]
                    tmat[r * sh : (r + 1) * sh, (base + k) * sw : (base + k + 1) * sw] = (
                        block * scale
                    ).astype(jnp.bfloat16)
        matched = jnp.dot(tmat[...], utab[...], preferred_element_type=jnp.float32)
        matched = matched.astype(jnp.bfloat16).astype(jnp.float32)
        place = jnp.full((1, width), -1, jnp.int32)
        for r in range(cap):
            p = picks[r]
            frac_rows = sub_pixel[0, p].astype(jnp.float32) * (1.0 / SUBSTEPS)
            frac_cols = sub_pixel[1, p].astype(jnp.float32) * (1.0 / SUBSTEPS)
            warped = bilinear(matched[r * sh : (r + 1) * sh, :], frac_rows, frac_cols)
            spread = bilinear(variance[p].astype(jnp.float32), frac_rows, frac_cols)
            weight = 1.0 / spread
            send_x[step, r * sh : (r + 1) * sh, 0:sw] = (weight * warped).astype(jnp.bfloat16)
            send_x[step, r * sh : (r + 1) * sh, sw : 2 * sw] = weight.astype(jnp.bfloat16)
            first = jnp.where(live[r], row_offset[p], -4 * TILE_ROWS)
            inside = (lane >= r * sh) & (lane < (r + 1) * sh)
            place = jnp.where(inside, first + lane - r * sh, place)
        send_m[step] = place

    def send_one(i, carry):
        step = tiles - 1 - i
        produce(step)
        data_copy(step).start()
        place_copy(step).start()
        return carry

    lax.fori_loop(0, tiles - 1, send_one, 0)
    produce(0)

    row_ids = lax.broadcasted_iota(jnp.int32, (TILE_ROWS, cap * sh), 0)

    def landed(block, place):
        picks = jnp.where(row_ids == place[:, : cap * sh], 1.0, 0.0).astype(jnp.bfloat16)
        return jnp.dot(picks, block, preferred_element_type=jnp.float32)

    acc[...] = landed(send_x[0], send_m[0])

    def take_one(i, carry):
        step = jnp.where(i < tiles // 2, i, tiles - 1 - (i - tiles // 2))
        data_copy(step).wait_recv()
        place_copy(step).wait_recv()
        acc[...] += landed(recv_x[step], recv_m[step])
        return carry

    lax.fori_loop(1, tiles, take_one, 0)

    def part_copy(q):
        return pltpu.make_async_remote_copy(
            src_ref=part_s.at[q], dst_ref=part_r.at[q],
            send_sem=sp_sem.at[q], recv_sem=rp_sem.at[q],
            device_id=owner_id(q)[1], device_id_type=MESH,
        )

    for q in range(1, owners):
        peer = owner_id(q)[0]
        start = pl.multiple_of(peer * own_rows, own_rows)
        part_s[q] = acc[pl.ds(start, own_rows), :].astype(jnp.bfloat16)
        part_copy(q).start()
    start = pl.multiple_of(mine * own_rows, own_rows)
    total = acc[pl.ds(start, own_rows), :]
    for q in range(1, owners):
        part_copy(q).wait_recv()
        total = total + part_r[q].astype(jnp.float32)
    out[...] = total[:, :sw] / (total[:, sw:] + 1.0)

    def drain(step, carry):
        data_copy(step).wait_send()
        place_copy(step).wait_send()
        return carry

    lax.fori_loop(1, tiles, drain, 0)
    for q in range(1, owners):
        part_copy(q).wait_send()


def paired_kernel(
    sizes,
    stamps_h, variance_h, basis_v_h, basis_u_h, coef_h, index_h, dest_h, offset_h, pixel_h,
    out,
    stamps, variance, basis_v, basis_u, coef, coef_index, tile_dest, row_offset, sub_pixel,
    taps_v, taps_u, vtab, utab, tmat, send_x, send_m, recv_x, recv_m, sum_s, sum_r, acc,
    in_sem, sx_sem, rx_sem, sm_sem, rm_sem, ss_sem, rs_sem,
):
    tiles, cap = sizes
    count, sh, sw = stamps.shape
    nb, tap_count = basis_v.shape
    half = (tap_count - 1) // 2
    pairs = tiles // 2
    own_rows = TILE_ROWS // 2
    rows = cap * sh
    me = lax.axis_index("tile")
    side = lax.axis_index("row") + lax.axis_index("band")
    group, core = lax.div(me, 2), lax.rem(me, 2)
    row_many = lax.axis_size("row") == 2

    def position(dx, dc):
        other = lax.rem(side + dx, 2)
        spot = {"tile": group * 2 + lax.rem(core + dc, 2)}
        spot["row" if row_many else "band"] = other
        return spot

    def far(step, dx):
        spot = {"tile": paired(group, step, pairs) * 2 + core}
        spot["row" if row_many else "band"] = lax.rem(side + dx, 2)
        return spot

    loads = start_loads(
        in_sem,
        (basis_v_h, basis_v), (basis_u_h, basis_u), (stamps_h, stamps), (coef_h, coef),
        (dest_h, tile_dest), (index_h, coef_index), (offset_h, row_offset),
        (pixel_h, sub_pixel), (variance_h, variance),
    )
    slots = [(dx, dc) for dx in range(2) for dc in range(2)]
    barrier = pltpu.get_barrier_semaphore()
    for dx, dc in slots[1:]:
        pl.semaphore_signal(barrier, inc=1, device_id=position(dx, dc), device_id_type=MESH)
    for step in range(1, pairs):
        for dx in range(2):
            pl.semaphore_signal(barrier, inc=1, device_id=far(step, dx), device_id_type=MESH)

    fill_tables(loads, basis_v, basis_u, taps_v, taps_u, vtab, utab, sh, sw)
    for load in loads[2:]:
        load.wait()

    width = send_m.shape[3]
    lane = lax.broadcasted_iota(jnp.int32, (1, width), 1)
    chunk = largest_divisor(nb, 3)
    exposure_ids = lax.broadcasted_iota(jnp.int32, coef.shape, 1)
    bilinear = bilinear_of(sh, sw)

    def group_copy(step, q):
        return pltpu.make_async_remote_copy(
            src_ref=send_x.at[step, q], dst_ref=recv_x.at[step, q],
            send_sem=sx_sem.at[step, q], recv_sem=rx_sem.at[step, q],
            device_id=position(*slots[q]), device_id_type=MESH,
        )

    def place_copy(step, q):
        return pltpu.make_async_remote_copy(
            src_ref=send_m.at[step, slots[q][1]], dst_ref=recv_m.at[step, q],
            send_sem=sm_sem.at[step, q], recv_sem=rm_sem.at[step, q],
            device_id=position(*slots[q]), device_id_type=MESH,
        )

    def sum_copy(step, dx):
        return pltpu.make_async_remote_copy(
            src_ref=sum_s.at[step, dx], dst_ref=sum_r.at[step, dx],
            send_sem=ss_sem.at[step, dx], recv_sem=rs_sem.at[step, dx],
            device_id=far(step, dx), device_id_type=MESH,
        )

    def send_sums(step):
        acc[...] = gathered(step)
        for dx in (1, 0):
            start = pl.multiple_of(lax.rem(side + dx, 2) * own_rows, own_rows)
            sum_s[step, dx] = acc[pl.ds(start, own_rows), :].astype(jnp.bfloat16)
            sum_copy(step, dx).start()

    def produce(step):
        base_tile = paired(group, step, pairs) * 2
        picks, live = [], []
        for dc in range(2):
            more, alive = listed_stamps(tile_dest, base_tile + lax.rem(core + dc, 2), count, cap)
            picks += more
            live += alive
        images = jnp.concatenate([stamps[p] for p in picks], axis=1)
        weights = [
            jnp.sum(jnp.where(exposure_ids == coef_index[p], coef[...], 0.0), axis=1, keepdims=True)
            for p in picks
        ]
        def across(first, last):
            return jnp.dot(
                tmat[:, first * sw : last * sw],
                utab[first * sw : last * sw, :],
                preferred_element_type=jnp.float32,
            )

        matched, done = None, 0
        for base in range(0, nb, chunk):
            ready = base - base % (2 * chunk)
            part = jnp.dot(
                vtab[base * sh : (base + chunk) * sh, :], images, preferred_element_type=jnp.float32
            )
            for k in range(chunk):
                for r in range(2 * cap):
                    block = part[k * sh : (k + 1) * sh, r * sw : (r + 1) * sw]
                    tmat[r * sh : (r + 1) * sh, (base + k) * sw : (base + k + 1) * sw] = (
                        block * weights[r][base + k : base + k + 1, :]
                    ).astype(jnp.bfloat16)
            if ready > done:
                term = across(done, ready)
                matched = term if matched is None else matched + term
                done = ready
        term = across(done, nb)
        matched = term if matched is None else matched + term
        matched = matched.astype(jnp.bfloat16).astype(jnp.float32)
        for dc in range(2):
            place = jnp.full((1, width), -4 * TILE_ROWS, jnp.int32)
            for r in range(cap):
                slot = dc * cap + r
                p = picks[slot]
                frac_rows = sub_pixel[0, p].astype(jnp.float32) * (1.0 / SUBSTEPS)
                frac_cols = sub_pixel[1, p].astype(jnp.float32) * (1.0 / SUBSTEPS)
                warped = bilinear(matched[slot * sh : (slot + 1) * sh, :], frac_rows, frac_cols)
                spread = bilinear(variance[p].astype(jnp.float32), frac_rows, frac_cols)
                weight = 1.0 / spread
                numer = weight * warped
                here = jnp.where(side == 0, numer, weight).astype(jnp.bfloat16)
                there = jnp.where(side == 0, weight, numer).astype(jnp.bfloat16)
                if dc == 0:
                    recv_x[step, 0, r * sh : (r + 1) * sh, :] = here
                else:
                    send_x[step, 1, r * sh : (r + 1) * sh, :] = here
                send_x[step, 2 + dc, r * sh : (r + 1) * sh, :] = there
                first = jnp.where(live[slot], row_offset[p], -4 * TILE_ROWS)
                inside = (lane >= r * sh) & (lane < (r + 1) * sh)
                place = jnp.where(inside, first + lane - r * sh, place)
            send_m[step, dc] = place
            if dc == 0:
                recv_m[step, 0] = place

    def send_group(step):
        for q in (2, 3, 1):
            group_copy(step, q).start()
            place_copy(step, q).start()

    middle = TILE_ROWS // 2
    row_ids = lax.broadcasted_iota(jnp.int32, (TILE_ROWS, rows), 0) - middle
    row_ids = row_ids.astype(jnp.float32).astype(jnp.bfloat16)
    one, zero = jnp.bfloat16(1.0), jnp.bfloat16(0.0)

    def gathered(step):
        total = None
        for q in (0, 1, 2, 3):
            if q > 0:
                group_copy(step, q).wait_recv()
                place_copy(step, q).wait_recv()
            place = (recv_m[step, q] - middle).astype(jnp.float32).astype(jnp.bfloat16)
            hit = jnp.where(row_ids == place[:, :rows], one, zero)
            part = jnp.dot(hit, recv_x[step, q], preferred_element_type=jnp.float32)
            total = part if total is None else total + part
        return total

    produce(pairs - 1)
    pl.semaphore_wait(barrier, len(slots) - 1 + 2 * (pairs - 1))
    send_group(pairs - 1)

    def one_step(i, carry):
        step = pairs - 1 - i
        produce(step)
        send_group(step)
        send_sums(step + 1)
        return carry

    lax.fori_loop(1, pairs, one_step, 0)
    acc[...] = gathered(0)
    start = pl.multiple_of((1 - side) * own_rows, own_rows)
    sum_s[0, 1] = acc[pl.ds(start, own_rows), :].astype(jnp.bfloat16)
    sum_copy(0, 1).start()
    own = acc[pl.ds(pl.multiple_of(side * own_rows, own_rows), own_rows), :]
    other = jnp.zeros_like(own)
    for step in range(pairs):
        if step > 0:
            sum_copy(step, 0).wait_recv()
            own = own + sum_r[step, 0].astype(jnp.float32)
        sum_copy(step, 1).wait_recv()
        other = other + sum_r[step, 1].astype(jnp.float32)
    out[...] = jnp.where(side == 0, own, other) / (jnp.where(side == 0, other, own) + 1.0)

    def drain(step, carry):
        for q in (1, 2, 3):
            group_copy(step, q).wait_send()
            place_copy(step, q).wait_send()
        return carry

    lax.fori_loop(0, pairs, drain, 0)
    for step in range(pairs):
        for dx in range(0 if step else 1, 2):
            sum_copy(step, dx).wait_send()


def local(
    stamps, variance, basis_v, basis_u, coefficients, coef_index, tile_dest, row_offset, sub_pixel
):
    tiles = lax.axis_size("tile")
    rows_n = lax.axis_size("row")
    bands = lax.axis_size("band")
    count, sh, sw = stamps.shape
    nb = basis_v.shape[0]
    cap = max(2, (count + tiles - 1) // tiles)
    owners = rows_n * bands
    own_rows = TILE_ROWS // owners
    width = -(-cap * sh // 128) * 128
    vmem = pl.BlockSpec(memory_space=pltpu.VMEM)
    anywhere = pl.BlockSpec(memory_space=pl.ANY)
    coefficients, sub_pixel = coefficients.T, sub_pixel.T
    big = [stamps, variance, basis_v, basis_u, coefficients]
    small = [coef_index, tile_dest, row_offset, sub_pixel]
    bf16, f32, dma = jnp.bfloat16, jnp.float32, pltpu.SemaphoreType.DMA
    inputs = [
        *(pltpu.VMEM(x.shape, x.dtype) for x in big),
        *(pltpu.SMEM(x.shape, x.dtype) for x in small),
        pltpu.VMEM((nb, sw), f32),
        pltpu.VMEM((nb, sw), f32),
        pltpu.VMEM((nb * sh, sh), bf16),
        pltpu.VMEM((nb * sw, sw), bf16),
    ]
    params = pltpu.CompilerParams(
        collective_id=0, has_side_effects=True, vmem_limit_bytes=56 * 1024 * 1024
    )
    if owners == 2 and tiles % 2 == 0 and tiles > 2:
        pairs = tiles // 2
        return pl.pallas_call(
            functools.partial(paired_kernel, (tiles, cap)),
            out_shape=jax.ShapeDtypeStruct((own_rows, sw), f32),
            in_specs=[anywhere] * 9,
            out_specs=vmem,
            scratch_shapes=[
                *inputs,
                pltpu.VMEM((2 * cap * sh, nb * sw), bf16),
                pltpu.VMEM((pairs, 4, cap * sh, sw), bf16),
                pltpu.VMEM((pairs, 2, 1, width), jnp.int32),
                pltpu.VMEM((pairs, 4, cap * sh, sw), bf16),
                pltpu.VMEM((pairs, 4, 1, width), jnp.int32),
                pltpu.VMEM((pairs, 2, own_rows, sw), bf16),
                pltpu.VMEM((pairs, 2, own_rows, sw), bf16),
                pltpu.VMEM((TILE_ROWS, sw), f32),
                dma((9,)),
                *(dma((pairs, 4)) for _ in range(4)),
                dma((pairs, 2)),
                dma((pairs, 2)),
            ],
            compiler_params=params,
        )(*big, *small)
    return pl.pallas_call(
        functools.partial(kernel, (tiles, rows_n, bands, cap)),
        out_shape=jax.ShapeDtypeStruct((own_rows, sw), f32),
        in_specs=[anywhere] * 9,
        out_specs=vmem,
        scratch_shapes=[
            *inputs,
            pltpu.VMEM((cap * sh, nb * sw), bf16),
            pltpu.VMEM((tiles, cap * sh, 2 * sw), bf16),
            pltpu.VMEM((tiles, 1, width), jnp.int32),
            pltpu.VMEM((tiles, cap * sh, 2 * sw), bf16),
            pltpu.VMEM((tiles, 1, width), jnp.int32),
            pltpu.VMEM((TILE_ROWS, 2 * sw), f32),
            pltpu.VMEM((owners, own_rows, 2 * sw), bf16),
            pltpu.VMEM((owners, own_rows, 2 * sw), bf16),
            pltpu.SemaphoreType.DMA((9,)),
            pltpu.SemaphoreType.DMA((tiles,)),
            pltpu.SemaphoreType.DMA((tiles,)),
            pltpu.SemaphoreType.DMA((tiles,)),
            pltpu.SemaphoreType.DMA((tiles,)),
            pltpu.SemaphoreType.DMA((owners,)),
            pltpu.SemaphoreType.DMA((owners,)),
        ],
        compiler_params=params,
    )(*big, *small)


def solution(mesh):
    in_specs = (
        P(("patch", "tile", "row", "band"), None, None),
        P(("patch", "tile", "row", "band"), None, None),
        P(),
        P(),
        P("patch", None),
        P(("patch", "tile", "row", "band")),
        P(("patch", "tile", "row", "band")),
        P(("patch", "tile", "row", "band")),
        P(("patch", "tile", "row", "band"), None),
    )
    out_specs = P(("patch", "tile", "row", "band"), None)
    return jax.shard_map(local, mesh=mesh, in_specs=in_specs, out_specs=out_specs, check_vma=False)
```
